32 devices in a mesh: dp: 8 (over z, x), rep: 4 (over y, core).
Axes of the slice: x: 2, y: 2, z: 4, core: 2. Of those that a mesh axis runs over, the one named last changes fastest.
Arguments:
- page_pool: bfloat16 [3584, 64, 576], P(('rep', 'dp')), parts along dimension 0, may hold values from -12 to 12
- move_source: int32 [768, 1], P('rep'), parts along dimension 0, may hold values from 0 to 7; in each aligned block of 24 rows (0 to 23, 24 to 47, ...) at most 5 rows name the same one
- move_page: int32 [768], P('rep'), parts along dimension 0, may hold values from 0 to 111
- move_slot: int32 [768], P('rep'), parts along dimension 0, may hold values from 0 to 111, as said below
- row_count: int32 [32], P(('rep', 'dp')), parts along dimension 0, may hold values from 1 to 16, as said below
- lengths: int32 [512], P(('rep', 'dp')), parts along dimension 0, may hold values from 1 to 2048, as said below
- page_table: int32 [512, 32], P(('rep', 'dp')), parts along dimension 0, may hold values from 0 to 111
- queries: bfloat16 [512, 64, 576], P(('rep', 'dp')), parts along dimension 0, may hold values from -32 to 32
- value_up: bfloat16 [64, 512, 128], P('dp'), may hold values from -0.25 to 0.25
- out_proj: bfloat16 [8192, 7168], P('dp'), may hold values from -0.375 to 0.375
- residual: bfloat16 [512, 7168], P(('rep', 'dp')), parts along dimension 0, may hold values from -6 to 6
- norm_gain: float32 [7168], replicated, may hold values from 0.1 to 1.9
- gate_proj: bfloat16 [7168, 9216], P(None, 'dp'), may hold values from -0.0625 to 0.0625
- up_proj: bfloat16 [7168, 9216], P(None, 'dp'), may hold values from -0.0625 to 0.0625
- down_proj: bfloat16 [9216, 7168], P('dp'), may hold values from -0.0625 to 0.0625
Outputs:
- layer_out: bfloat16 [512, 7168], P(('rep', 'dp')), parts along dimension 0
The draws below stay inside these ranges and needn't reach their ends.
There are 4 independent parts, one for each index of `rep`. The reference program is written for one: setup_inputs(seed, part) draws one part's arguments, and reference() takes and returns one part's arrays. A program takes and returns all parts, laid end to end along the dimension named above; an argument that names none is the same for every part. Nothing has to cross between parts.
Inputs may be any that keep to these rules, and one draw needn't show every extreme that they name: `move_source`: within the 24 moves of one destination rank, no source rank appears more than 5 times, and some source appears exactly 5 times. `move_slot`: the 24 slots of one destination rank are distinct. `row_count`: some rank has exactly 16 live rows. `lengths`: some row has exactly 2048 tokens.
All inputs are finite; a program needn't handle non-finite values.
Results may differ from the reference program's by a relative error of at most 0.02.
Values may be sent and summed in bfloat16 or wider, within the bound.
No kernel may reach another device: no remote copies, remote signals or barrier semaphores. Data moves between devices by JAX's collectives and lax.ppermute only.
A program may use at most 128 MiB of HBM per device.

```python
import math
import jax
import jax.numpy as jnp
import numpy as np
from jax import lax

D = 7168
FF = 9216
HEADS = 64
LATENT = 512
ROPE = 64
VDIM = 128
PAGE = 64
POOL = 112
MAXP = 32
ROWS_MAX = 16
MOVES = 24
CAP = 5
ROWS = 128
N_DP = 8


def draw_page_pool(key, part):
    key = jax.random.fold_in(key, 1)
    shape = (N_DP * POOL, PAGE, LATENT + ROPE)
    values = jax.random.normal(key, shape, jnp.float32)
    return jnp.clip(values, -12.0, 12.0).astype(jnp.bfloat16)


def draw_queries(key, part):
    key = jax.random.fold_in(key, 2)
    shape = (N_DP * ROWS_MAX, HEADS, LATENT + ROPE)
    values = 0.5 * jax.random.normal(key, shape, jnp.float32)
    return jnp.clip(values, -32.0, 32.0).astype(jnp.bfloat16)


def draw_move_slot(key, part):
    key = jax.random.fold_in(key, 3)
    row_keys = jax.random.split(key, N_DP)
    slots = jax.vmap(lambda row_key: jax.random.permutation(row_key, POOL)[:MOVES])(row_keys)
    return slots.reshape(-1).astype(jnp.int32)


def draw_row_count(key, part):
    key = jax.random.fold_in(key, 4)
    counts = jax.random.randint(key, (N_DP,), 1, ROWS_MAX + 1)
    fullest = jax.random.randint(jax.random.fold_in(key, 1), (), 0, N_DP)
    return jnp.where(jnp.arange(N_DP) == fullest, ROWS_MAX, counts).astype(jnp.int32)


def draw_lengths(key, part):
    key = jax.random.fold_in(key, 6)
    values = jax.random.randint(key, (N_DP * ROWS_MAX,), 1, MAXP * PAGE + 1)
    longest = jax.random.randint(jax.random.fold_in(key, 1), (), 0, N_DP * ROWS_MAX)
    return jnp.where(jnp.arange(N_DP * ROWS_MAX) == longest, MAXP * PAGE, values).astype(jnp.int32)


def touch_ends(array, stream_key, low, largest):
    index_at = [jax.random.randint(jax.random.fold_in(stream_key, axis), (), 0, length) for axis, length in enumerate(array.shape)]
    widest = array.shape.index(max(array.shape))
    next_to = index_at[:widest] + [(index_at[widest] + 1) % array.shape[widest]] + index_at[widest + 1:]
    return array.at[tuple(index_at)].set(low).at[tuple(next_to)].set(largest)


def shard_levels(rng, extent, shards, least, high):
    factor_of = 1.0
    for axis_at, parts in shards:
        heights = jax.random.uniform(jax.random.fold_in(jax.random.fold_in(rng, 6), axis_at), (parts,), jnp.float32, least / len(shards), high / len(shards))
        factor_of = factor_of * jnp.repeat(jnp.exp(heights), extent[axis_at] // parts).reshape((-1,) + (1,) * (len(extent) - 1 - axis_at))
    return factor_of


def shared_out(own_key, own, number, rows, number_of, top, limit, lean):
    sequence = jax.random.permutation(own_key, number_of)
    heavy_load, common = portions_of(number_of, rows * top, limit, lean, True), portions_of(number_of, rows * top, limit, lean, False)
    places = jnp.arange(number_of)

    def named(tallies, offset_by):
        used = int((tallies > 0).sum())
        fixed = max(1, used // 4)
        passed = fixed + (places - fixed + offset_by * (used - fixed)) % max(1, number_of - fixed)
        return jnp.zeros((number_of,), jnp.int32).at[sequence[jnp.where(places < fixed, places, passed)]].set(jnp.asarray(tallies, jnp.int32))

    tallies = jnp.where(number % 4 == 0, named(heavy_load, number // 4), named(common, number - number // 4 - 1))
    mixed = jax.random.permutation(jax.random.fold_in(own, 3), number_of)
    source_of, sink = mixed[0:number_of // 2 * 2:2], mixed[1:number_of // 2 * 2:2]
    margin = jnp.minimum(tallies[source_of] - 1, limit - tallies[sink]) // 2
    margin = jnp.where((source_of == sequence[0]) | (sink == sequence[0]) | (tallies[sink] == 0), 0, jnp.maximum(margin, 0))
    passed = jax.random.randint(jax.random.fold_in(own, 4), (number_of // 2,), 0, 1 << 20) % (margin + 1)
    tallies = tallies.at[source_of].add(-passed).at[sink].add(passed)
    labels = jnp.searchsorted(jnp.cumsum(tallies), jnp.arange(rows * top), side="right").astype(jnp.int32)
    listing = labels.reshape(top, rows).T
    listing = listing[jax.random.permutation(jax.random.fold_in(own, 1), rows)]
    offset_by = jax.random.randint(jax.random.fold_in(own, 2), (rows, 1), 0, top)
    return jnp.take_along_axis(listing, (jnp.arange(top)[None, :] + offset_by) % top, axis=1)


def portions_of(count, total, most, slope, full):
    weights = [(1 << 20) // math.isqrt(grade ** slope) + 1 for grade in range(1, count + 1)]
    largest = most if full else min(most, max(-(-total // count), total * weights[0] // sum(weights)))
    least = 1 if total - largest >= count - 1 else 0
    holding, rest = [largest] + [least] * (count - 1), total - largest - least * (count - 1)
    while rest > 0:
        movable = [i for i in range(1, count) if holding[i] < largest] or [i for i in range(1, count) if holding[i] < most]
        pool, budget = sum([weights[i] for i in movable]), rest
        for i in movable:
            addition = min(most - holding[i], max(1, budget * weights[i] // pool), rest)
            holding[i] = holding[i] + addition
            rest = rest - addition
    return np.array(holding)


def centred(own_key, shape, spread, reach, cuts=(), dtype=jnp.bfloat16):
    gain = shard_levels(own_key, shape, cuts, -0.22, 0.18) if cuts else 1.0
    values = jax.random.normal(own_key, shape, jnp.float32) * spread * gain
    return jnp.minimum(jnp.maximum(values, -reach), reach).astype(dtype)


def setup_inputs(seed: int = 0, part: int = 0) -> dict:
    splits = jax.random.split(jax.random.key(seed), 16)
    own_keys = jax.random.split(jax.random.fold_in(splits[15], part), 16)
    page_pool = draw_page_pool(jax.random.fold_in(jax.random.fold_in(splits[15], part), 71), part)
    move_source_keys = jax.random.split(jax.random.fold_in(own_keys[1], 1), (N_DP * MOVES) // MOVES)
    move_source_turns = jax.random.permutation(jax.random.fold_in(own_keys[1], 3), (N_DP * MOVES) // MOVES)
    move_source = jax.vmap(lambda own, number: shared_out(jax.random.fold_in(own_keys[1], 2), own, number, MOVES, N_DP, 1, CAP, 2))(move_source_keys, move_source_turns).reshape((N_DP * MOVES, 1))
    move_page = touch_ends(jax.random.randint(own_keys[2], (N_DP * MOVES,), 0, POOL), jax.random.fold_in(own_keys[2], 1), 0, POOL - 1).astype(jnp.int32)
    move_slot = draw_move_slot(jax.random.fold_in(jax.random.fold_in(splits[15], part), 71), part)
    row_count = draw_row_count(jax.random.fold_in(jax.random.fold_in(splits[15], part), 71), part)
    lengths = draw_lengths(jax.random.fold_in(jax.random.fold_in(splits[15], part), 71), part)
    page_table = touch_ends(jax.random.randint(own_keys[6], (ROWS, MAXP), 0, POOL), jax.random.fold_in(own_keys[6], 1), 0, POOL - 1).astype(jnp.int32)
    queries = draw_queries(jax.random.fold_in(jax.random.fold_in(splits[15], part), 71), part)
    value_up = centred(splits[8], (HEADS, LATENT, VDIM), LATENT ** -0.5, 0.25, ((0, 8),))
    out_proj = centred(splits[9], (HEADS * VDIM, D), (HEADS * VDIM // 32) ** -0.5, 0.375, ((0, 8),))
    residual = centred(own_keys[10], (ROWS, D), 1.0, 6.0, ((0, 8),))
    norm_gain = jnp.clip(1.0 + 0.18 * jax.random.normal(splits[11], (D,), jnp.float32), 0.1, 1.9)
    gate_proj = centred(splits[12], (D, FF), D ** -0.5, 0.0625, ((1, 8),))
    up_proj = centred(splits[13], (D, FF), D ** -0.5, 0.0625, ((1, 8),))
    down_proj = centred(splits[14], (FF, D), FF ** -0.5, 0.0625, ((0, 8),))
    return dict(page_pool=page_pool, move_source=move_source, move_page=move_page, move_slot=move_slot, row_count=row_count, lengths=lengths, page_table=page_table, queries=queries, value_up=value_up, out_proj=out_proj, residual=residual, norm_gain=norm_gain, gate_proj=gate_proj, up_proj=up_proj, down_proj=down_proj)


SOFTMAX_SCALE = 192 ** (-0.5)

def rms_scale(values, gain_row):
    factor = lax.rsqrt(lax.optimization_barrier(jnp.mean(values * values, axis=-1, keepdims=True)) + 1e-06)
    return (values * factor * gain_row).astype(jnp.bfloat16)

def attend_rank(cache_pages, tables, row_lens, queries, row_limit):

    def one_row(inputs):
        table_row, row_len, query_row = inputs
        tokens = cache_pages[table_row].reshape(-1, cache_pages.shape[2])
        scores = jnp.einsum('hk,tk->ht', query_row.astype(jnp.float32), tokens.astype(jnp.float32)) * SOFTMAX_SCALE
        live_mask = jnp.arange(tokens.shape[0]) < row_len
        scores = jnp.where(live_mask[None, :], scores, -jnp.inf)
        top_score = lax.optimization_barrier(jnp.max(scores, axis=1, keepdims=True))
        exponent = jnp.exp(scores - top_score)
        weights = (exponent / lax.optimization_barrier(jnp.sum(exponent, axis=1, keepdims=True))).astype(jnp.bfloat16)
        latent_part = tokens[:, :LATENT].astype(jnp.float32)
        return jnp.einsum('ht,tl->hl', weights.astype(jnp.float32), latent_part).astype(jnp.bfloat16)
    outputs = lax.map(one_row, (tables, row_lens, queries))
    valid_rows = jnp.arange(tables.shape[0]) < row_limit
    return jnp.where(valid_rows[:, None, None], outputs, jnp.zeros_like(outputs))

def reference(page_pool, move_source, move_page, move_slot, row_count, lengths, page_table, queries, value_up, out_proj, residual, norm_gain, gate_proj, up_proj, down_proj):
    blocks = page_pool.reshape(N_DP, POOL, PAGE, LATENT + ROPE)
    sources = move_source.reshape(N_DP, MOVES).astype(jnp.int32)
    page_ids = move_page.reshape(N_DP, MOVES).astype(jnp.int32)
    slot_ids = move_slot.reshape(N_DP, MOVES).astype(jnp.int32)
    carried = blocks[sources, page_ids]
    moved_pool = jax.vmap(lambda pages_block, slot_list, fresh_pages: pages_block.at[slot_list].set(fresh_pages))(blocks, slot_ids, carried)

    def per_rank(packed):
        return attend_rank(*packed)
    latent_out = lax.map(per_rank, (moved_pool, page_table.reshape(N_DP, ROWS_MAX, MAXP), lengths.reshape(N_DP, ROWS_MAX), queries.reshape(N_DP, ROWS_MAX, HEADS, LATENT + ROPE), row_count))
    latent_out = latent_out.reshape(N_DP * ROWS_MAX, HEADS, LATENT)
    head_out = jnp.einsum('rhl,hlv->rhv', latent_out.astype(jnp.float32), value_up.astype(jnp.float32)).astype(jnp.bfloat16)
    head_out = head_out.reshape(N_DP * ROWS_MAX, HEADS * VDIM)
    middle = residual.astype(jnp.float32) + jnp.dot(head_out, out_proj, preferred_element_type=jnp.float32)
    normed = rms_scale(middle, norm_gain)
    gate_part = jnp.dot(normed, gate_proj, preferred_element_type=jnp.float32)
    up_part = jnp.dot(normed, up_proj, preferred_element_type=jnp.float32)
    hidden = (jax.nn.silu(gate_part) * up_part).astype(jnp.bfloat16)
    return (middle + jnp.dot(hidden, down_proj, preferred_element_type=jnp.float32)).astype(jnp.bfloat16)
```

```python
import functools
import math

import jax
import jax.numpy as jnp
from jax import lax
from jax.experimental import pallas as pl
from jax.experimental.pallas import tpu as pltpu
from jax.sharding import PartitionSpec as P

LATENT = 512
SOFTMAX_SCALE = 192 ** (-0.5)
LOG2_SCALE = SOFTMAX_SCALE * math.log2(math.e)
MASKED = -1e30
MIB = 1 << 20
CHUNKS = 2


def in_hbm(array):
    return pltpu.with_memory_space_constraint(array, pltpu.HBM)


def in_vmem(array):
    return pltpu.with_memory_space_constraint(array, pltpu.VMEM)


def pack_kernel(peers, near, capacity, ids_ref, rank_ref, pool_ref, _, *refs):
    out_refs, (pages_ref, sems) = refs[:-2], refs[-2:]
    if near:
        out_refs = [out_refs[0].at[k] for k in range(len(peers))]
    own = rank_ref[0]
    page_size = pages_ref.shape[1]
    half = page_size // 2
    slots = [(k, c) for k in range(len(peers)) for c in range(capacity)]

    def copy(n):
        k, c = slots[n]
        peer = (own & ~(len(peers) - 1)) + k if near else own ^ peers[k]
        page = ids_ref[peer * capacity + c]
        return pltpu.make_async_copy(pool_ref.at[page], pages_ref.at[n], sems.at[n])

    for n in range(len(slots)):
        copy(n).start()
    for n, (k, c) in enumerate(slots):
        copy(n).wait()
        for block in range(LATENT // 128):
            out_refs[k][c, pl.ds(block * page_size, page_size), :] = pages_ref[
                n, :, pl.ds(block * 128, 128)
            ]
        rope = pages_ref[n, :, LATENT:]
        out_refs[k][c, pl.ds(LATENT // 128 * page_size, half), :] = jnp.concatenate(
            [rope[:half], rope[half:]], axis=1
        )


def pack_pages(page_pool, ids, rank, peers, near, capacity, after):
    page_size, width = page_pool.shape[1:]
    shape = (capacity, page_size * width // 128, 128)
    count = len(peers) * capacity
    shapes = [(len(peers),) + shape] if near else [shape] * len(peers)
    return pl.pallas_call(
        functools.partial(pack_kernel, tuple(peers), near, capacity),
        out_shape=[jax.ShapeDtypeStruct(shape, page_pool.dtype) for shape in shapes],
        grid_spec=pltpu.PrefetchScalarGridSpec(
            num_scalar_prefetch=2,
            grid=(),
            in_specs=[pl.BlockSpec(memory_space=pltpu.HBM), pl.BlockSpec(memory_space=pl.ANY)],
            out_specs=[pl.BlockSpec(memory_space=pltpu.VMEM)] * len(shapes),
            scratch_shapes=[
                pltpu.VMEM((count, page_size, width), page_pool.dtype),
                pltpu.SemaphoreType.DMA((count,)),
            ],
        ),
        compiler_params=pltpu.CompilerParams(vmem_limit_bytes=16 * MIB),
        name="pack_near" if near else "pack_far",
    )(ids, rank, in_hbm(page_pool), after)


def unpack_pages(packed_refs, tokens_ref, page_size):
    half = page_size // 2
    width = tokens_ref.shape[1] - LATENT
    at = 0
    for packed_ref in packed_refs:
        for c in range(packed_ref.shape[0]):
            span = pl.ds(at, page_size)
            for block in range(LATENT // 128):
                tokens_ref[span, pl.ds(block * 128, 128)] = packed_ref[
                    c, pl.ds(block * page_size, page_size), :
                ]
            rope = packed_ref[c, pl.ds(LATENT // 128 * page_size, half), :]
            tokens_ref[span, LATENT:] = jnp.concatenate([rope[:, :width], rope[:, width:]], axis=0)
            at += page_size


def token_bias(counts, first_page, tokens, page_size):
    whole, last, part = counts
    rows, slots = whole.shape
    shift = page_size.bit_length() - 1
    page = (lax.broadcasted_iota(jnp.int32, (slots, tokens), 1) >> shift) + first_page
    spread = jnp.where(
        page == lax.broadcasted_iota(jnp.int32, (slots, tokens), 0), 1.0, 0.0
    ).astype(jnp.bfloat16)
    times = jnp.dot(whole, spread, preferred_element_type=jnp.float32)
    ends = jnp.dot(last, spread, preferred_element_type=jnp.float32)
    offset = lax.broadcasted_iota(jnp.int32, (rows, tokens), 1) & (page_size - 1)
    times = times + jnp.where(offset < part, ends, 0.0)
    return jnp.where(times > 0.5, jnp.log2(jnp.maximum(times, 1.0)), MASKED)


def absorb(raw, tokens, bias, state):
    top, total, acc = state
    rows, count = bias.shape
    scores = (raw.reshape(-1, rows, count) * LOG2_SCALE + bias[None]).reshape(-1, count)
    new_top = jnp.maximum(top, jnp.max(scores, axis=1, keepdims=True))
    weights = jnp.exp2(scores - new_top)
    shrink = jnp.exp2(top - new_top)
    total = total * shrink + jnp.sum(weights, axis=1, keepdims=True)
    acc = acc * shrink + jnp.dot(
        weights.astype(jnp.bfloat16), tokens[:, :LATENT], preferred_element_type=jnp.float32
    )
    return new_top, total, acc


def attend(q_ref, tokens, bias, states):
    size = q_ref.shape[0] // len(states)
    raw = [
        lax.dot_general(
            q_ref[pl.ds(i * size, size), :],
            tokens,
            (((1,), (1,)), ((), ())),
            preferred_element_type=jnp.float32,
        )
        for i in range(len(states))
    ]
    return [absorb(scores, tokens, bias, state) for scores, state in zip(raw, states)]


PARTS = 2


def store_state(states, refs):
    stats_ref, acc_ref = refs
    half = stats_ref.shape[1] // 2
    for i, (top, total, acc) in enumerate(states):
        span = pl.ds(i * acc.shape[0], acc.shape[0])
        stats_ref[span, :] = jnp.concatenate(
            [jnp.broadcast_to(x, (x.shape[0], half)) for x in (top, total)], axis=1
        )
        acc_ref[span, :] = acc


def load_state(refs):
    stats_ref, acc_ref = refs
    half = stats_ref.shape[1] // 2
    size = acc_ref.shape[0] // PARTS
    spans = [pl.ds(i * size, size) for i in range(PARTS)]
    return [
        (stats_ref[span, :1], stats_ref[span, half : half + 1], acc_ref[span, :]) for span in spans
    ]


def counts_of(refs):
    return tuple(ref[...] for ref in refs)


def resident_kernel(
    chunk, page_size, whole_ref, last_ref, part_ref, q_ref, pool_ref, *refs
):
    state_refs, (tokens_ref, bias_ref, sem) = refs[:2], refs[2:]
    token_count = tokens_ref.shape[0]
    count = q_ref.shape[0] // PARTS

    @pl.when(pl.program_id(0) == 0)
    def _():
        copy = pltpu.make_async_copy(pool_ref, tokens_ref, sem)
        copy.start()
        counts = counts_of((whole_ref, last_ref, part_ref))
        for first in range(0, token_count, chunk):
            bias_ref[:, pl.ds(first, chunk)] = token_bias(
                counts, first // page_size, chunk, page_size
            )
        copy.wait()

    def step(index, state):
        span = pl.ds(pl.multiple_of(index * chunk, chunk), chunk)
        return attend(q_ref, tokens_ref[span, :], bias_ref[:, span], state)

    empty = (
        jnp.full((count, 1), MASKED, jnp.float32),
        jnp.zeros((count, 1), jnp.float32),
        jnp.zeros((count, LATENT), jnp.float32),
    )
    states = lax.fori_loop(0, token_count // chunk, step, [empty] * PARTS)
    store_state(states, state_refs)


def state_layout(count, group, block):
    widths = (128, LATENT)
    shapes = tuple(pltpu.HBM((count, w), jnp.float32) for w in widths)
    specs = tuple(pl.BlockSpec((group, w), block) for w in widths)
    return shapes, specs


def attend_resident(queries, pool, counts, page_size, group=512, chunk=1024):
    count, width = queries.shape
    token_count = pool.shape[0]
    rows = counts[0].shape[0]
    block = lambda g: (g, 0)
    fixed = lambda g: (0, 0)
    shapes, specs = state_layout(count, group, block)
    return pl.pallas_call(
        functools.partial(resident_kernel, chunk, page_size),
        out_shape=shapes,
        grid=(count // group,),
        in_specs=[pl.BlockSpec(array.shape, fixed) for array in counts]
        + [pl.BlockSpec((group, width), block), pl.BlockSpec(memory_space=pltpu.HBM)],
        out_specs=specs,
        scratch_shapes=[
            pltpu.VMEM((token_count, width), pool.dtype),
            pltpu.VMEM((rows, token_count), jnp.float32),
            pltpu.SemaphoreType.DMA,
        ],
        compiler_params=pltpu.CompilerParams(vmem_limit_bytes=32 * MIB),
        cost_estimate=pl.CostEstimate(
            flops=2 * count * token_count * (width + LATENT),
            bytes_accessed=2 * token_count * width + 4 * count * LATENT,
            transcendentals=count * token_count,
        ),
        name="attend_resident",
    )(*counts, queries, in_hbm(pool))


def near_kernel(pages, place, page_size, whole_ref, last_ref, part_ref, q_ref, *refs):
    packed_refs, refs = refs[:pages], refs[pages:]
    before, after, (tokens_ref, bias_ref) = refs[:2], refs[2:4], refs[4:]

    @pl.when(pl.program_id(0) == 0)
    def _():
        unpack_pages(packed_refs, tokens_ref, page_size)
        counts = counts_of((whole_ref, last_ref, part_ref))
        bias_ref[...] = token_bias(counts, place, tokens_ref.shape[0], page_size)

    store_state(attend(q_ref, tokens_ref[...], bias_ref[...], load_state(before)), after)


def arrival_operands(packed, counts, fixed):
    once = pl.Buffered(1)
    count_specs = [pl.BlockSpec(array.shape, fixed) for array in counts]
    page_specs = [
        pl.BlockSpec(p.shape, lambda *_: (0, 0, 0), pipeline_mode=once) for p in packed
    ]
    tokens = sum(p.shape[0] for p in packed)
    return count_specs, page_specs, tokens


def attend_near(queries, packed, counts, place, state, page_size, group=512):
    count, width = queries.shape
    block = lambda g: (g, 0)
    count_specs, page_specs, pages = arrival_operands(packed, counts, lambda g: (0, 0))
    tokens = pages * page_size
    shapes, specs = state_layout(count, group, block)
    return pl.pallas_call(
        functools.partial(near_kernel, len(packed), place, page_size),
        out_shape=shapes,
        grid=(count // group,),
        in_specs=count_specs + [pl.BlockSpec((group, width), block)] + page_specs + list(specs),
        out_specs=specs,
        scratch_shapes=[
            pltpu.VMEM((tokens, width), queries.dtype),
            pltpu.VMEM((counts[0].shape[0], tokens), jnp.float32),
        ],
        compiler_params=pltpu.CompilerParams(vmem_limit_bytes=24 * MIB),
        cost_estimate=pl.CostEstimate(
            flops=2 * count * tokens * (width + LATENT),
            bytes_accessed=2 * tokens * width + 8 * count * LATENT,
            transcendentals=count * tokens,
        ),
        name="attend_near",
    )(*counts, queries, *packed, *map(in_hbm, state))


def latents_of(limit_ref, q_ref, tokens, bias, before):
    states = attend(q_ref, tokens, bias, load_state(before))
    latent = jnp.concatenate([acc / total for _, total, acc in states], axis=0)
    latent = latent.reshape(-1, bias.shape[0], LATENT)
    live = lax.broadcasted_iota(jnp.int32, latent.shape, 1) < limit_ref[0]
    return jnp.where(live, latent, 0.0).reshape(-1, LATENT).astype(jnp.bfloat16)


def latents_far_kernel(pages, place, page_size, rank_ref, limit_ref, *refs):
    count_refs, q_ref, refs = refs[:3], refs[3], refs[4:]
    packed_refs, before, refs = refs[:pages], refs[pages : pages + 2], refs[pages + 2 :]
    out_refs, (tokens_ref, bias_ref, latent_ref) = refs[:-3], refs[-3:]
    unpack_pages(packed_refs, tokens_ref, page_size)
    bias_ref[...] = token_bias(counts_of(count_refs), place, tokens_ref.shape[0], page_size)
    latent_ref[...] = latents_of(limit_ref, q_ref, tokens_ref[...], bias_ref[...], before)
    sharing, size = len(out_refs), out_refs[0].shape[0]
    for u, out_ref in enumerate(out_refs):
        at = pl.multiple_of(((rank_ref[0] & (sharing - 1)) ^ u) * size, size)
        out_ref[...] = latent_ref[pl.ds(at, size), :]


def latents_near_kernel(rank_ref, limit_ref, q_ref, tokens_ref, bias_ref, *refs):
    before, out_ref = refs[:2], refs[2]
    out_ref[...] = latents_of(limit_ref, q_ref, tokens_ref[...], bias_ref[...], before)


def latents(queries, packed, counts, place, state, rank, limit, page_size, ranks):
    count, width = queries.shape
    half, size = ranks // 2, count // ranks
    tokens = sum(p.shape[0] for p in packed) * page_size
    own = lambda g, rank, _: (lax.div(rank[0], half), 0)
    other = lambda g, rank, _: (1 - lax.div(rank[0], half), 0)
    fixed = lambda g, *_: (0, 0)
    state_shapes = ((count // 2, 128), (count // 2, LATENT))
    state_specs = lambda block: [pl.BlockSpec(shape, block) for shape in state_shapes]
    array = jax.ShapeDtypeStruct
    options = dict(
        compiler_params=pltpu.CompilerParams(vmem_limit_bytes=28 * MIB),
        cost_estimate=pl.CostEstimate(
            flops=count * tokens * (width + LATENT),
            bytes_accessed=2 * tokens * width + 2 * count * LATENT,
            transcendentals=count * tokens // 2,
        ),
    )
    state = [in_hbm(x) for x in state]
    *far, unpacked, bias = pl.pallas_call(
        functools.partial(latents_far_kernel, len(packed), place, page_size),
        out_shape=[array((size, LATENT), jnp.bfloat16)] * half
        + [array((tokens, width), queries.dtype), array((counts[0].shape[0], tokens), jnp.float32)],
        grid_spec=pltpu.PrefetchScalarGridSpec(
            num_scalar_prefetch=2,
            grid=(1,),
            in_specs=[pl.BlockSpec(x.shape, fixed) for x in counts]
            + [pl.BlockSpec((count // 2, width), other)]
            + [pl.BlockSpec(p.shape, lambda *_: (0, 0, 0)) for p in packed]
            + state_specs(other),
            out_specs=[pl.BlockSpec((size, LATENT), fixed)] * half
            + [pl.BlockSpec((tokens, width), fixed)]
            + [pl.BlockSpec((counts[0].shape[0], tokens), fixed)],
            scratch_shapes=[pltpu.VMEM((count // 2, LATENT), jnp.bfloat16)],
        ),
        name="latents_far",
        **options,
    )(rank, limit, *counts, queries, *packed, *state)
    near = pl.pallas_call(
        latents_near_kernel,
        out_shape=pltpu.HBM((count // 2, LATENT), jnp.bfloat16),
        grid_spec=pltpu.PrefetchScalarGridSpec(
            num_scalar_prefetch=2,
            grid=(1,),
            in_specs=[pl.BlockSpec((count // 2, width), own)]
            + [pl.BlockSpec(x.shape, fixed) for x in (unpacked, bias)]
            + state_specs(own),
            out_specs=pl.BlockSpec((count // 2, LATENT), fixed),
        ),
        name="latents_near",
        **options,
    )(rank, limit, queries, unpacked, bias, *state)
    return far, near


def slot_counts(content, lengths, slots, page_size):
    full = lengths // page_size
    order = jnp.arange(content.shape[1])
    same = content[:, :, None] == slots[None, None, :]
    whole = jnp.sum((same & (order < full[:, None])[:, :, None]).astype(jnp.float32), axis=1)
    last = jnp.sum((same & (order == full[:, None])[:, :, None]).astype(jnp.float32), axis=1)
    return whole.astype(jnp.bfloat16), last.astype(jnp.bfloat16), (lengths % page_size)[:, None]


def stream(weight_ref, tiles_ref, sems, row, column):
    count, depth, width = tiles_ref.shape
    along_rows = depth < weight_ref.shape[0]
    copies = []
    for n in range(count):
        rows = pl.ds(row + (n * depth if along_rows else 0), depth)
        columns = pl.ds(column + (0 if along_rows else n * width), width)
        copies.append(
            pltpu.make_async_copy(weight_ref.at[rows, columns], tiles_ref.at[n], sems.at[n])
        )
    for copy in copies:
        copy.start()
    return copies


def multiply_tiles(places, rows_ref, tiles_ref, copies, keep_ref, send_ref):
    half, width = keep_ref.shape[0], tiles_ref.shape[2]
    size = 2 * half // len(places)
    for n, copy in enumerate(copies):
        copy.wait()
        product = jnp.dot(
            rows_ref[...], tiles_ref[n], preferred_element_type=jnp.float32
        ).astype(jnp.bfloat16)
        for to, at in enumerate(places):
            out_ref, to = (keep_ref, to * size) if to * size < half else (send_ref, to * size - half)
            out_ref[pl.ds(to, size), pl.ds(n * width, width)] = product[at * size : (at + 1) * size]


def project_first_kernel(column, order, rank_ref, near_ref, *refs):
    split = near_ref.shape[0]
    far_refs, refs = refs[:split], refs[split:]
    value_ref, weight_ref, head_ref, keep_ref, send_ref, tiles_ref, sems = refs
    copies = stream(weight_ref, tiles_ref, sems, 0, column)
    own = rank_ref[0] & (split - 1)
    parts = [near_ref.at[own ^ k] for k in range(split)] + list(far_refs)
    heads, width = value_ref.shape[0], value_ref.shape[2]
    slots = near_ref.shape[1] // heads
    for h in range(heads):
        rows = jnp.concatenate([parts[k][pl.ds(h * slots, slots), :] for k in order], axis=0)
        head_ref[:, pl.ds(h * width, width)] = jnp.dot(
            rows, value_ref[h], preferred_element_type=jnp.float32
        ).astype(jnp.bfloat16)
    multiply_tiles(range(len(order)), head_ref, tiles_ref, copies, keep_ref, send_ref)


def project_kernel(column, places, rows_ref, weight_ref, keep_ref, send_ref, tiles_ref, sems):
    copies = stream(weight_ref, tiles_ref, sems, 0, column)
    multiply_tiles(places, rows_ref, tiles_ref, copies, keep_ref, send_ref)


def project_options(rows, depth, columns, tile):
    return dict(
        scratch_shapes=[
            pltpu.VMEM((columns // tile, depth, tile), jnp.bfloat16),
            pltpu.SemaphoreType.DMA((columns // tile,)),
        ],
        compiler_params=pltpu.CompilerParams(vmem_limit_bytes=20 * MIB),
        cost_estimate=pl.CostEstimate(
            flops=2 * rows * depth * columns,
            bytes_accessed=2 * depth * columns + 2 * rows * (columns + depth),
            transcendentals=0,
        ),
    )


def project_first(order, rank, near, far, value_up, weight, columns, tile=512):
    depth = weight.shape[0]
    rows = len(order) * near.shape[1] // value_up.shape[0]
    vmem = pl.BlockSpec(memory_space=pltpu.VMEM)
    half = jax.ShapeDtypeStruct((rows // 2, columns), jnp.bfloat16)
    return pl.pallas_call(
        functools.partial(project_first_kernel, 0, order),
        out_shape=(jax.ShapeDtypeStruct((rows, depth), jnp.bfloat16), half, half),
        in_specs=[pl.BlockSpec(memory_space=pltpu.SMEM)]
        + [vmem] * (len(far) + 2)
        + [pl.BlockSpec(memory_space=pltpu.HBM)],
        name="project_first",
        **project_options(rows, depth, columns, tile),
    )(rank, near, *far, value_up, in_hbm(weight))


def project(rows, weight, columns, chunk, places, name, tile=512):
    count, depth = rows.shape
    half = jax.ShapeDtypeStruct((count // 2, columns), jnp.bfloat16)
    return pl.pallas_call(
        functools.partial(project_kernel, chunk * columns, tuple(places)),
        out_shape=(half, half),
        in_specs=[
            pl.BlockSpec(memory_space=pltpu.VMEM),
            pl.BlockSpec(memory_space=pltpu.HBM),
        ],
        name=name,
        **project_options(count, depth, columns, tile),
    )(rows, in_hbm(weight))


def halve_kernel(keep_ref, came_ref, own_ref, send_ref):
    total = keep_ref[...].astype(jnp.float32) + came_ref[...].astype(jnp.float32)
    half = own_ref.shape[0]
    own_ref[...] = total[:half]
    send_ref[...] = total[half:].astype(send_ref.dtype)


def halve(keep, came):
    shape = (keep.shape[0] // 2, keep.shape[1])
    return pl.pallas_call(
        halve_kernel,
        out_shape=(
            jax.ShapeDtypeStruct(shape, jnp.float32),
            jax.ShapeDtypeStruct(shape, jnp.bfloat16),
        ),
        compiler_params=pltpu.CompilerParams(vmem_limit_bytes=16 * MIB),
        name="halve",
    )(keep, came)


def finish_kernel(residual_ref, gain_ref, own_ref, *refs):
    others, (middle_ref, scaled_ref) = refs[:-2], refs[-2:]
    middle = residual_ref[...].astype(jnp.float32) + own_ref[...]
    for other in others:
        middle = middle + other[...].astype(jnp.float32)
    middle_ref[...] = middle
    scaled_ref[...] = (middle * gain_ref[...]).astype(scaled_ref.dtype)


def finish_middle(residual, gain, sums, chunk):
    rows, columns = sums[0].shape
    here = lambda _: (0, chunk)
    block = pl.BlockSpec((rows, columns), lambda _: (0, 0))
    return pl.pallas_call(
        finish_kernel,
        out_shape=(
            jax.ShapeDtypeStruct((rows, columns), jnp.float32),
            jax.ShapeDtypeStruct((rows, columns), jnp.bfloat16),
        ),
        grid=(1,),
        in_specs=[pl.BlockSpec((rows, columns), here), pl.BlockSpec((1, columns), here)]
        + [block] * len(sums),
        out_specs=(block, block),
        compiler_params=pltpu.CompilerParams(vmem_limit_bytes=16 * MIB),
        name="finish_middle",
    )(residual, gain, *sums)


def gather_matmul_kernel(row, first, last, n_pieces, places, mean_over, *refs):
    pieces, refs = refs[:n_pieces], refs[n_pieces:]
    inverse_ref, gate_ref, up_ref, refs = refs[0], refs[1], refs[2], refs[3:]
    before, refs = ((), refs) if first else (refs[:3], refs[3:])
    if last:
        hidden_ref, gate_acc, up_acc, squares, *refs = refs
    else:
        gate_acc, up_acc, squares, *refs = refs
    (rows_ref,) = refs
    steps, _, depth = rows_ref.shape
    size = pieces[0].shape[0]
    sources = [(piece, b) for piece in pieces for b in range(piece.shape[0] // size)]
    for (piece, b), place in zip(sources, places):
        for k in range(steps):
            rows_ref[k, pl.ds(place * size, size), :] = piece[
                pl.ds(b * size, size), pl.ds(k * depth, depth)
            ]
    for now, old in zip((gate_acc, up_acc, squares), before):
        now[...] = old[...]

    for k in range(steps):
        rows = rows_ref[k]
        plain = rows.astype(jnp.float32) * inverse_ref[:, pl.ds(k * depth, depth)]
        square = jnp.broadcast_to(jnp.sum(plain * plain, axis=1, keepdims=True), squares.shape)
        span = pl.ds(row + k * depth, depth)
        gate = jnp.dot(rows, gate_ref[span, :], preferred_element_type=jnp.float32)
        up = jnp.dot(rows, up_ref[span, :], preferred_element_type=jnp.float32)
        if first and k == 0:
            squares[...], gate_acc[...], up_acc[...] = square, gate, up
        else:
            squares[...] += square
            gate_acc[...] += gate
            up_acc[...] += up

    if last:
        factor = lax.rsqrt(squares[:, :1] / mean_over + 1e-06)
        gate = gate_acc[...] * factor
        hidden_ref[...] = (gate * jax.nn.sigmoid(gate) * (up_acc[...] * factor)).astype(
            jnp.bfloat16
        )


def gather_matmul(
    pieces, places, inverse_gain, gate_proj, up_proj, before, chunk, last, tile=512
):
    columns = pieces[0].shape[1]
    rows = sum(piece.shape[0] for piece in pieces)
    width, units = gate_proj.shape
    steps = columns // tile
    sums = ((rows, units), (rows, units), (rows, 128))
    if last:
        out_shape = jax.ShapeDtypeStruct((rows, units), jnp.bfloat16)
        scratch = [pltpu.VMEM(shape, jnp.float32) for shape in sums]
    else:
        out_shape = tuple(jax.ShapeDtypeStruct(shape, jnp.float32) for shape in sums)
        scratch = []
    vmem = pl.BlockSpec(memory_space=pltpu.VMEM)
    return pl.pallas_call(
        functools.partial(
            gather_matmul_kernel,
            chunk * columns,
            before is None,
            last,
            len(pieces),
            tuple(places),
            width,
        ),
        out_shape=out_shape,
        in_specs=[vmem] * (len(pieces) + 3 + len(before or ())),
        scratch_shapes=scratch + [pltpu.VMEM((steps, rows, tile), jnp.bfloat16)],
        compiler_params=pltpu.CompilerParams(vmem_limit_bytes=12 * MIB),
        cost_estimate=pl.CostEstimate(
            flops=4 * rows * columns * units,
            bytes_accessed=4 * columns * units + 2 * rows * columns,
            transcendentals=0,
        ),
        name="gate_up",
    )(*pieces, inverse_gain, in_vmem(gate_proj), in_vmem(up_proj), *(before or ()))


class Grid:
    def __init__(self, count):
        self.count = count
        self.bits = count.bit_length() - 1

    def dims(self, chunk):
        first = [1, 0] if chunk % 2 else [0, 1]
        return first + list(range(2, self.bits))

    def order(self, chunk):
        dims = self.dims(chunk)
        return [
            sum(1 << d for i, d in enumerate(dims) if n >> (self.bits - 1 - i) & 1)
            for n in range(self.count)
        ]

    def places(self, chunk):
        base = self.order(0)
        return [base.index(k) for k in self.order(chunk)]

    def exchange(self, array, k):
        return lax.ppermute(array, "dp", [(i, i ^ k) for i in range(self.count)])

    def exchange_near(self, array):
        half = self.count // 2
        groups = [list(range(half)), list(range(half, self.count))]
        return lax.all_to_all(
            array, "dp", split_axis=0, concat_axis=0, axis_index_groups=groups, tiled=True
        )

    def scatter_sum(self, keep, send, chunk):
        *before, last = self.dims(chunk)
        for d in before:
            keep, send = halve(keep, self.exchange(send, 1 << d))
        return [keep, self.exchange(send, 1 << last)]

    def gather(self, block, chunk):
        pieces = [block]
        for d in reversed(self.dims(chunk)):
            held = jnp.concatenate(pieces, axis=0) if len(pieces) > 1 else block
            pieces.append(self.exchange(held, 1 << d))
        return pieces


def add_up(base, parts):
    for part in parts:
        base = base + part.astype(jnp.float32)
    return base


def body(
    page_pool,
    move_source,
    move_page,
    move_slot,
    row_count,
    lengths,
    page_table,
    queries,
    value_up,
    out_proj,
    residual,
    norm_gain,
    gate_proj,
    up_proj,
    down_proj,
):
    rank_count = lax.axis_size("dp")
    own_rank = lax.axis_index("dp")
    grid = Grid(rank_count)
    rank = own_rank[None]
    move_count = move_page.shape[0] // rank_count
    capacity = max(2, (3 * move_count + 2 * rank_count - 1) // (2 * rank_count))
    slot_count, page_size, feature_width = page_pool.shape
    sources = move_source.T.reshape(rank_count, move_count)
    page_ids = move_page.reshape(rank_count, move_count)
    slot_ids = move_slot.reshape(rank_count, move_count)
    move_order = jnp.arange(move_count)
    earlier = (sources[:, :, None] == sources[:, None, :]) & (
        move_order[None, None, :] < move_order[None, :, None]
    )
    arrival = jnp.sum(earlier.astype(jnp.int32), axis=2)
    chosen = (sources == own_rank)[:, :, None] & (
        arrival[:, :, None] == jnp.arange(capacity)[None, None, :]
    )
    send_ids = jnp.sum(jnp.where(chosen, page_ids[:, :, None], 0), axis=1).reshape(-1)
    split = rank_count // 2
    far_peers = range(split, rank_count)
    packed = pack_pages(page_pool, send_ids, rank, far_peers, False, capacity, rank)
    far_pages = [grid.exchange(pages, k) for k, pages in zip(far_peers, packed)]
    (packed,) = pack_pages(page_pool, send_ids, rank, range(split), True, capacity, packed[0])
    near_pages = grid.exchange_near(packed)

    pick = lambda array: lax.dynamic_index_in_dim(array, own_rank, 0, keepdims=False)
    own_slots, own_pages = pick(slot_ids), pick(page_ids)
    peer = pick(sources) ^ own_rank
    place = jnp.where(peer < split, pick(sources) & (split - 1), peer) * capacity + pick(arrival)
    content_of = jnp.where(peer == 0, own_pages, slot_count + place)
    hit = page_table[:, :, None] == own_slots[None, None, :]
    content = jnp.where(
        jnp.any(hit, axis=2), jnp.sum(jnp.where(hit, content_of, 0), axis=2), page_table
    )
    places = slot_count + rank_count * capacity
    counts = slot_counts(content, lengths, jnp.arange(places), page_size)
    far_place = slot_count + split * capacity

    row_slots, head_count = queries.shape[:2]
    by_head_queries = queries.transpose(1, 0, 2).reshape(head_count * row_slots, feature_width)
    state = attend_resident(
        by_head_queries,
        page_pool.reshape(slot_count * page_size, feature_width),
        counts,
        page_size,
    )
    near_pages = near_pages.reshape((split * capacity,) + near_pages.shape[2:])
    state = attend_near(by_head_queries, [near_pages], counts, slot_count, state, page_size)
    far_latents, near_latents = latents(
        by_head_queries,
        far_pages,
        counts,
        far_place,
        state,
        rank,
        row_count,
        page_size,
        rank_count,
    )
    far_latents = [grid.exchange(x, k) for k, x in zip(far_peers, far_latents)]
    near_latents = grid.exchange_near(near_latents.reshape(split, -1, LATENT))

    width = residual.shape[1]
    columns = width // CHUNKS
    head_out, *halves = project_first(
        grid.order(0), rank, near_latents, far_latents, value_up, out_proj, columns
    )
    projected = [halves] + [
        project(head_out, out_proj, columns, c, grid.places(c), "project_out")
        for c in range(1, CHUNKS)
    ]
    middle, gathered = [], []
    for c, (keep, send) in enumerate(projected):
        row_sum, scaled = finish_middle(
            residual, norm_gain[None, :], grid.scatter_sum(keep, send, c), c
        )
        middle.append(row_sum)
        gathered.append(grid.gather(scaled, c))
    inverse_gain = (1.0 / norm_gain)[None, :]
    sums = None
    for c, pieces in enumerate(gathered):
        span = slice(c * columns, (c + 1) * columns)
        sums = gather_matmul(
            pieces,
            grid.places(c),
            inverse_gain[:, span],
            gate_proj,
            up_proj,
            sums,
            c,
            c == CHUNKS - 1,
        )
    hidden = sums
    outputs = []
    for c in range(CHUNKS):
        keep, send = project(hidden, down_proj, columns, c, grid.places(c), "project_down")
        outputs.append(add_up(middle[c], grid.scatter_sum(keep, send, c)).astype(jnp.bfloat16))
    return jnp.concatenate(outputs, axis=1)


def solution(mesh):
    in_specs = (
        P(("rep", "dp"), None, None),
        P("rep", None),
        P("rep"),
        P("rep"),
        P(("rep", "dp")),
        P(("rep", "dp")),
        P(("rep", "dp"), None),
        P(("rep", "dp"), None, None),
        P("dp", None, None),
        P("dp", None),
        P(("rep", "dp"), None),
        P(),
        P(None, "dp"),
        P(None, "dp"),
        P("dp", None),
    )
    out_specs = P(("rep", "dp"), None)
    return jax.shard_map(body, mesh=mesh, in_specs=in_specs, out_specs=out_specs, check_vma=False)
```

```python
import functools
import math

import jax
import jax.numpy as jnp
from jax import lax
from jax.experimental import pallas as pl
from jax.experimental.pallas import tpu as pltpu
from jax.sharding import PartitionSpec as P

LATENT = 512
SOFTMAX_SCALE = 192 ** (-0.5)
LOG2_SCALE = SOFTMAX_SCALE * math.log2(math.e)
MASKED = -1e30
MIB = 1 << 20
CHUNKS = 2
SMALL = pl.CostEstimate(flops=1, bytes_accessed=1, transcendentals=0)


def in_hbm(array):
    return pltpu.with_memory_space_constraint(array, pltpu.HBM)


def in_vmem(array):
    return pltpu.with_memory_space_constraint(array, pltpu.VMEM)


def pack_kernel(peers, near, capacity, moves, source_ref, page_ref, rank_ref, pool_ref, _, *refs):
    out_refs, (pages_ref, sems) = refs[:-2], refs[-2:]
    if near:
        out_refs = [out_refs[0].at[k] for k in range(len(peers))]
    own = rank_ref[0]
    page_size = pages_ref.shape[1]
    half = page_size // 2

    def copy(page, place):
        return pltpu.make_async_copy(pool_ref.at[page], pages_ref.at[place], sems.at[place])

    counts = []
    for k, peer in enumerate(peers):
        first = ((own & ~(len(peers) - 1)) + k if near else own ^ peer) * moves

        def look(i, count, k=k, first=first):
            chosen = (source_ref[0, first + i] == own) & (count < capacity)

            @pl.when(chosen)
            def _():
                copy(page_ref[first + i], k * capacity + count).start()

            return count + chosen.astype(jnp.int32)

        counts.append(lax.fori_loop(0, moves, look, jnp.int32(0)))
    for k in range(len(peers)):
        for c in range(capacity):
            place, out_ref = k * capacity + c, out_refs[k]

            @pl.when(c < counts[k])
            def _(c=c, place=place, out_ref=out_ref):
                copy(0, place).wait()
                for block in range(LATENT // 128):
                    out_ref[c, pl.ds(block * page_size, page_size), :] = pages_ref[
                        place, :, pl.ds(block * 128, 128)
                    ]
                rope = pages_ref[place, :, LATENT:]
                out_ref[c, pl.ds(LATENT // 128 * page_size, half), :] = jnp.concatenate(
                    [rope[:half], rope[half:]], axis=1
                )

            @pl.when(c >= counts[k])
            def _(c=c, out_ref=out_ref):
                out_ref[c] = jnp.zeros(out_ref.shape[1:], out_ref.dtype)


def pack_pages(page_pool, sources, pages, rank, ranks, peers, near, capacity, after):
    page_size, width = page_pool.shape[1:]
    shape = (capacity, page_size * width // 128, 128)
    count = len(peers) * capacity
    shapes = [(len(peers),) + shape] if near else [shape] * len(peers)
    smem = pl.BlockSpec(memory_space=pltpu.SMEM)
    return pl.pallas_call(
        functools.partial(pack_kernel, tuple(peers), near, capacity, pages.shape[0] // ranks),
        out_shape=[jax.ShapeDtypeStruct(shape, page_pool.dtype) for shape in shapes],
        in_specs=[
            smem,
            smem,
            smem,
            pl.BlockSpec(memory_space=pltpu.HBM),
            pl.BlockSpec(memory_space=pl.ANY),
        ],
        out_specs=[pl.BlockSpec(memory_space=pltpu.VMEM)] * len(shapes),
        scratch_shapes=[
            pltpu.VMEM((count, page_size, width), page_pool.dtype),
            pltpu.SemaphoreType.DMA((count,)),
        ],
        compiler_params=pltpu.CompilerParams(vmem_limit_bytes=8 * MIB),
        name="pack_near" if near else "pack_far",
    )(sources, pages, rank, in_hbm(page_pool), after)


def unpack_pages(packed_refs, tokens_ref, page_size):
    half = page_size // 2
    width = tokens_ref.shape[1] - LATENT
    at = 0
    for packed_ref in packed_refs:
        for c in range(packed_ref.shape[0]):
            span = pl.ds(at, page_size)
            for block in range(LATENT // 128):
                tokens_ref[span, pl.ds(block * 128, 128)] = packed_ref[
                    c, pl.ds(block * page_size, page_size), :
                ]
            rope = packed_ref[c, pl.ds(LATENT // 128 * page_size, half), :]
            tokens_ref[span, LATENT:] = jnp.concatenate([rope[:, :width], rope[:, width:]], axis=0)
            at += page_size


def token_bias(counts, first_page, tokens, page_size):
    whole, last, part = counts
    rows, slots = whole.shape
    shift = page_size.bit_length() - 1
    page = (lax.broadcasted_iota(jnp.int32, (slots, tokens), 1) >> shift) + first_page
    spread = jnp.where(
        page == lax.broadcasted_iota(jnp.int32, (slots, tokens), 0), 1.0, 0.0
    ).astype(jnp.bfloat16)
    times = jnp.dot(whole, spread, preferred_element_type=jnp.float32)
    ends = jnp.dot(last, spread, preferred_element_type=jnp.float32)
    offset = lax.broadcasted_iota(jnp.int32, (rows, tokens), 1) & (page_size - 1)
    times = times + jnp.where(offset < part, ends, 0.0)
    return jnp.where(times > 0.5, jnp.log2(jnp.maximum(times, 1.0)), MASKED)


def absorb(raw, tokens, bias, state):
    top, total, acc = state
    rows, count = bias.shape
    scores = (raw.reshape(-1, rows, count) * LOG2_SCALE + bias[None]).reshape(-1, count)
    new_top = jnp.maximum(top, jnp.max(scores, axis=1, keepdims=True))
    weights = jnp.exp2(scores - new_top)
    shrink = jnp.exp2(top - new_top)
    total = total * shrink + jnp.sum(weights, axis=1, keepdims=True)
    acc = acc * shrink + jnp.dot(
        weights.astype(jnp.bfloat16), tokens[:, :LATENT], preferred_element_type=jnp.float32
    )
    return new_top, total, acc


def attend(q_ref, tokens, bias, states):
    size = q_ref.shape[0] // len(states)
    raw = [
        lax.dot_general(
            q_ref[pl.ds(i * size, size), :],
            tokens,
            (((1,), (1,)), ((), ())),
            preferred_element_type=jnp.float32,
        )
        for i in range(len(states))
    ]
    return [absorb(scores, tokens, bias, state) for scores, state in zip(raw, states)]


PARTS = 2


def store_state(states, refs):
    stats_ref, acc_ref = refs
    half = stats_ref.shape[1] // 2
    for i, (top, total, acc) in enumerate(states):
        span = pl.ds(i * acc.shape[0], acc.shape[0])
        stats_ref[span, :] = jnp.concatenate(
            [jnp.broadcast_to(x, (x.shape[0], half)) for x in (top, total)], axis=1
        )
        acc_ref[span, :] = acc


def load_state(refs):
    stats_ref, acc_ref = refs
    half = stats_ref.shape[1] // 2
    size = acc_ref.shape[0] // PARTS
    spans = [pl.ds(i * size, size) for i in range(PARTS)]
    return [
        (stats_ref[span, :1], stats_ref[span, half : half + 1], acc_ref[span, :]) for span in spans
    ]


def counts_of(refs):
    return tuple(ref[...] for ref in refs)


def resident_kernel(
    chunk, page_size, whole_ref, last_ref, part_ref, q_ref, pool_ref, *refs
):
    state_refs, (tokens_ref, bias_ref, sem) = refs[:2], refs[2:]
    token_count = tokens_ref.shape[0]
    count = q_ref.shape[0] // PARTS

    @pl.when(pl.program_id(0) == 0)
    def _():
        copy = pltpu.make_async_copy(pool_ref, tokens_ref, sem)
        copy.start()
        counts = counts_of((whole_ref, last_ref, part_ref))
        for first in range(0, token_count, chunk):
            bias_ref[:, pl.ds(first, chunk)] = token_bias(
                counts, first // page_size, chunk, page_size
            )
        copy.wait()

    def step(index, state):
        span = pl.ds(pl.multiple_of(index * chunk, chunk), chunk)
        return attend(q_ref, tokens_ref[span, :], bias_ref[:, span], state)

    empty = (
        jnp.full((count, 1), MASKED, jnp.float32),
        jnp.zeros((count, 1), jnp.float32),
        jnp.zeros((count, LATENT), jnp.float32),
    )
    states = lax.fori_loop(0, token_count // chunk, step, [empty] * PARTS)
    store_state(states, state_refs)


def state_layout(count, group, block):
    widths = (128, LATENT)
    shapes = tuple(pltpu.HBM((count, w), jnp.float32) for w in widths)
    specs = tuple(pl.BlockSpec((group, w), block) for w in widths)
    return shapes, specs


def attend_resident(queries, pool, counts, page_size, group=512, chunk=1024):
    count, width = queries.shape
    token_count = pool.shape[0]
    rows = counts[0].shape[0]
    block = lambda g: (g, 0)
    fixed = lambda g: (0, 0)
    shapes, specs = state_layout(count, group, block)
    return pl.pallas_call(
        functools.partial(resident_kernel, chunk, page_size),
        out_shape=shapes,
        grid=(count // group,),
        in_specs=[pl.BlockSpec(array.shape, fixed) for array in counts]
        + [pl.BlockSpec((group, width), block), pl.BlockSpec(memory_space=pltpu.HBM)],
        out_specs=specs,
        scratch_shapes=[
            pltpu.VMEM((token_count, width), pool.dtype),
            pltpu.VMEM((rows, token_count), jnp.float32),
            pltpu.SemaphoreType.DMA,
        ],
        compiler_params=pltpu.CompilerParams(vmem_limit_bytes=32 * MIB),
        cost_estimate=SMALL,
        name="attend_resident",
    )(*counts, queries, in_hbm(pool))


def near_kernel(pages, place, page_size, whole_ref, last_ref, part_ref, q_ref, *refs):
    packed_refs, refs = refs[:pages], refs[pages:]
    before, after, (tokens_ref, bias_ref) = refs[:2], refs[2:4], refs[4:]

    @pl.when(pl.program_id(0) == 0)
    def _():
        unpack_pages(packed_refs, tokens_ref, page_size)
        counts = counts_of((whole_ref, last_ref, part_ref))
        bias_ref[...] = token_bias(counts, place, tokens_ref.shape[0], page_size)

    store_state(attend(q_ref, tokens_ref[...], bias_ref[...], load_state(before)), after)


def arrival_operands(packed, counts, fixed):
    once = pl.Buffered(1)
    count_specs = [pl.BlockSpec(array.shape, fixed) for array in counts]
    page_specs = [
        pl.BlockSpec(p.shape, lambda *_: (0, 0, 0), pipeline_mode=once) for p in packed
    ]
    tokens = sum(p.shape[0] for p in packed)
    return count_specs, page_specs, tokens


def attend_near(queries, packed, counts, place, state, page_size, group=512):
    count, width = queries.shape
    block = lambda g: (g, 0)
    count_specs, page_specs, pages = arrival_operands(packed, counts, lambda g: (0, 0))
    tokens = pages * page_size
    shapes, specs = state_layout(count, group, block)
    return pl.pallas_call(
        functools.partial(near_kernel, len(packed), place, page_size),
        out_shape=shapes,
        grid=(count // group,),
        in_specs=count_specs + [pl.BlockSpec((group, width), block)] + page_specs + list(specs),
        out_specs=specs,
        scratch_shapes=[
            pltpu.VMEM((tokens, width), queries.dtype),
            pltpu.VMEM((counts[0].shape[0], tokens), jnp.float32),
        ],
        compiler_params=pltpu.CompilerParams(vmem_limit_bytes=24 * MIB),
        cost_estimate=SMALL,
        name="attend_near",
    )(*counts, queries, *packed, *map(in_hbm, state))


def latents_of(limit_ref, q_ref, tokens, bias, before):
    states = attend(q_ref, tokens, bias, load_state(before))
    latent = jnp.concatenate([acc / total for _, total, acc in states], axis=0)
    latent = latent.reshape(-1, bias.shape[0], LATENT)
    live = lax.broadcasted_iota(jnp.int32, latent.shape, 1) < limit_ref[0]
    return jnp.where(live, latent, 0.0).reshape(-1, LATENT).astype(jnp.bfloat16)


def latents_far_kernel(pages, place, page_size, rank_ref, limit_ref, *refs):
    count_refs, q_ref, refs = refs[:3], refs[3], refs[4:]
    packed_refs, before, refs = refs[:pages], refs[pages : pages + 2], refs[pages + 2 :]
    out_refs, (tokens_ref, bias_ref, latent_ref) = refs[:-3], refs[-3:]
    unpack_pages(packed_refs, tokens_ref, page_size)
    bias_ref[...] = token_bias(counts_of(count_refs), place, tokens_ref.shape[0], page_size)
    latent_ref[...] = latents_of(limit_ref, q_ref, tokens_ref[...], bias_ref[...], before)
    sharing, size = len(out_refs), out_refs[0].shape[0]
    for u, out_ref in enumerate(out_refs):
        at = pl.multiple_of(((rank_ref[0] & (sharing - 1)) ^ u) * size, size)
        out_ref[...] = latent_ref[pl.ds(at, size), :]


def latents_near_kernel(rank_ref, limit_ref, q_ref, tokens_ref, bias_ref, *refs):
    before, out_ref = refs[:2], refs[2]
    out_ref[...] = latents_of(limit_ref, q_ref, tokens_ref[...], bias_ref[...], before)


def latents(queries, packed, counts, place, state, rank, limit, page_size, ranks, exchange):
    count, width = queries.shape
    half, size = ranks // 2, count // ranks
    tokens = sum(p.shape[0] for p in packed) * page_size
    own = lambda g, rank, _: (lax.div(rank[0], half), 0)
    other = lambda g, rank, _: (1 - lax.div(rank[0], half), 0)
    fixed = lambda g, *_: (0, 0)
    state_specs = lambda block: [pl.BlockSpec((count // 2, w), block) for w in (128, LATENT)]
    array = jax.ShapeDtypeStruct
    options = dict(
        compiler_params=pltpu.CompilerParams(vmem_limit_bytes=24 * MIB),
        cost_estimate=pl.CostEstimate(
            flops=count * tokens * (width + LATENT),
            bytes_accessed=2 * tokens * width + 2 * count * LATENT,
            transcendentals=count * tokens // 2,
        ),
    )
    state = [in_hbm(x) for x in state]
    *far, unpacked, bias = pl.pallas_call(
        functools.partial(latents_far_kernel, len(packed), place, page_size),
        out_shape=[array((size, LATENT), jnp.bfloat16)] * half
        + [array((tokens, width), queries.dtype), array((counts[0].shape[0], tokens), jnp.float32)],
        grid_spec=pltpu.PrefetchScalarGridSpec(
            num_scalar_prefetch=2,
            grid=(1,),
            in_specs=[pl.BlockSpec(x.shape, fixed) for x in counts]
            + [pl.BlockSpec((count // 2, width), other)]
            + [pl.BlockSpec(p.shape, lambda *_: (0, 0, 0)) for p in packed]
            + state_specs(other),
            out_specs=[pl.BlockSpec((size, LATENT), fixed)] * half
            + [pl.BlockSpec((tokens, width), fixed)]
            + [pl.BlockSpec((counts[0].shape[0], tokens), fixed)],
            scratch_shapes=[pltpu.VMEM((count // 2, LATENT), jnp.bfloat16)],
        ),
        name="latents_far",
        **options,
    )(rank, limit, *counts, queries, *packed, *state)
    far = [exchange(block, half + u) for u, block in enumerate(far)]
    near = pl.pallas_call(
        latents_near_kernel,
        out_shape=pltpu.HBM((count // 2, LATENT), jnp.bfloat16),
        grid_spec=pltpu.PrefetchScalarGridSpec(
            num_scalar_prefetch=2,
            grid=(1,),
            in_specs=[pl.BlockSpec((count // 2, width), own)]
            + [pl.BlockSpec(x.shape, fixed) for x in (unpacked, bias)]
            + state_specs(own),
            out_specs=pl.BlockSpec((count // 2, LATENT), fixed),
        ),
        name="latents_near",
        **dict(options, cost_estimate=SMALL),
    )(rank, limit, queries, unpacked, bias, *state)
    return far, near


def slot_counts(content, lengths, slots, page_size):
    full = lengths // page_size
    order = jnp.arange(content.shape[1])
    same = content[:, :, None] == slots[None, None, :]
    whole = jnp.sum((same & (order < full[:, None])[:, :, None]).astype(jnp.float32), axis=1)
    last = jnp.sum((same & (order == full[:, None])[:, :, None]).astype(jnp.float32), axis=1)
    return whole.astype(jnp.bfloat16), last.astype(jnp.bfloat16), (lengths % page_size)[:, None]


def multiply_tiles(places, tiles, rows_ref, keep_ref, send_ref):
    half, columns = keep_ref.shape
    size, tile = 2 * half // len(places), columns // len(tiles)
    for n, load in enumerate(tiles):
        product = jnp.dot(rows_ref[...], load(), preferred_element_type=jnp.float32)
        product = product.astype(jnp.bfloat16)
        for to, at in enumerate(places):
            out_ref, to = (keep_ref, to * size) if to * size < half else (send_ref, to * size - half)
            out_ref[pl.ds(to, size), pl.ds(n * tile, tile)] = product[at * size : (at + 1) * size]


def stream(weight_ref, tiles_ref, sems, column):
    width = tiles_ref.shape[2]
    copies = [
        pltpu.make_async_copy(
            weight_ref.at[:, pl.ds(column + n * width, width)], tiles_ref.at[n], sems.at[n]
        )
        for n in range(tiles_ref.shape[0])
    ]
    for copy in copies:
        copy.start()

    def load(n):
        copies[n].wait()
        return tiles_ref[n]

    return [functools.partial(load, n) for n in range(len(copies))]


def project_first_kernel(order, rank_ref, near_ref, *refs):
    split = len(order) // 2
    far, refs = refs[:split], refs[split:]
    value_ref, weight_ref, head_ref, keep_ref, send_ref, tiles_ref, sems = refs
    tiles = stream(weight_ref, tiles_ref, sems, 0)
    heads, width = value_ref.shape[0], value_ref.shape[2]
    own, slots = rank_ref[0] & (split - 1), near_ref.shape[1] // heads
    for h in range(heads):
        span = pl.ds(h * slots, slots)
        rows = jnp.concatenate(
            [near_ref[own ^ k, span, :] if k < split else far[k - split][span, :] for k in order],
            axis=0,
        )
        head_ref[:, pl.ds(h * width, width)] = jnp.dot(
            rows, value_ref[h], preferred_element_type=jnp.float32
        ).astype(jnp.bfloat16)
    multiply_tiles(range(len(order)), tiles, head_ref, keep_ref, send_ref)


def project_kernel(column, places, rows_ref, weight_ref, keep_ref, send_ref, tiles_ref, sems):
    multiply_tiles(places, stream(weight_ref, tiles_ref, sems, column), rows_ref, keep_ref, send_ref)


def project_options(rows, depth, columns, tile):
    return dict(
        scratch_shapes=[
            pltpu.VMEM((columns // tile, depth, tile), jnp.bfloat16),
            pltpu.SemaphoreType.DMA((columns // tile,)),
        ],
        compiler_params=pltpu.CompilerParams(vmem_limit_bytes=12 * MIB),
        cost_estimate=pl.CostEstimate(
            flops=2 * rows * depth * columns,
            bytes_accessed=2 * depth * columns + 2 * rows * (columns + depth),
            transcendentals=0,
        ),
    )


def project_first(order, rank, near, far, value_up, weight, columns, tile=512):
    depth = weight.shape[0]
    rows = len(order) * near.shape[1] // value_up.shape[0]
    half = jax.ShapeDtypeStruct((rows // 2, columns), jnp.bfloat16)
    vmem = pl.BlockSpec(memory_space=pltpu.VMEM)
    return pl.pallas_call(
        functools.partial(project_first_kernel, order),
        out_shape=(jax.ShapeDtypeStruct((rows, depth), jnp.bfloat16), half, half),
        in_specs=[pl.BlockSpec(memory_space=pltpu.SMEM)]
        + [vmem] * (2 + len(far))
        + [pl.BlockSpec(memory_space=pltpu.HBM)],
        name="project_first",
        **project_options(rows, depth, columns, tile),
    )(rank, near, *far, value_up, in_hbm(weight))


def project(rows, weight, columns, chunk, places, name, tile=512):
    count, depth = rows.shape
    half = jax.ShapeDtypeStruct((count // 2, columns), jnp.bfloat16)
    return pl.pallas_call(
        functools.partial(project_kernel, chunk * columns, tuple(places)),
        out_shape=(half, half),
        in_specs=[pl.BlockSpec(memory_space=pltpu.VMEM), pl.BlockSpec(memory_space=pltpu.HBM)],
        name=name,
        **project_options(count, depth, columns, tile),
    )(rows, in_hbm(weight))


def halve_kernel(keep_ref, came_ref, own_ref, send_ref):
    total = keep_ref[...].astype(jnp.float32) + came_ref[...].astype(jnp.float32)
    half = own_ref.shape[0]
    own_ref[...] = total[:half]
    send_ref[...] = total[half:].astype(send_ref.dtype)


def halve(keep, came):
    shape = (keep.shape[0] // 2, keep.shape[1])
    return pl.pallas_call(
        halve_kernel,
        out_shape=(
            jax.ShapeDtypeStruct(shape, jnp.float32),
            jax.ShapeDtypeStruct(shape, jnp.bfloat16),
        ),
        compiler_params=pltpu.CompilerParams(vmem_limit_bytes=6 * MIB),
        name="halve",
    )(keep, came)


def finish_kernel(residual_ref, gain_ref, own_ref, *refs):
    others, (middle_ref, scaled_ref) = refs[:-2], refs[-2:]
    middle = residual_ref[...].astype(jnp.float32) + own_ref[...]
    for other in others:
        middle = middle + other[...].astype(jnp.float32)
    middle_ref[...] = middle
    scaled_ref[...] = (middle * gain_ref[...]).astype(scaled_ref.dtype)


def finish_middle(residual, gain, sums, chunk):
    rows, columns = sums[0].shape
    here = lambda _: (0, chunk)
    block = pl.BlockSpec((rows, columns), lambda _: (0, 0))
    return pl.pallas_call(
        finish_kernel,
        out_shape=(
            jax.ShapeDtypeStruct((rows, columns), jnp.float32),
            jax.ShapeDtypeStruct((rows, columns), jnp.bfloat16),
        ),
        grid=(1,),
        in_specs=[pl.BlockSpec((rows, columns), here), pl.BlockSpec((1, columns), here)]
        + [block] * len(sums),
        out_specs=(block, block),
        compiler_params=pltpu.CompilerParams(vmem_limit_bytes=4 * MIB),
        name="finish_middle",
    )(residual, gain, *sums)


def gather_matmul_kernel(row, first, last, n_pieces, places, mean_over, *refs):
    pieces, refs = refs[:n_pieces], refs[n_pieces:]
    inverse_ref, gate_ref, up_ref, refs = refs[0], refs[1], refs[2], refs[3:]
    before, refs = ((), refs) if first else (refs[:3], refs[3:])
    if last:
        hidden_ref, gate_acc, up_acc, squares, *refs = refs
    else:
        gate_acc, up_acc, squares, *refs = refs
    rows_ref, tiles_ref, sems = refs
    steps, _, depth = rows_ref.shape
    copies = [
        pltpu.make_async_copy(
            up_ref.at[pl.ds(row + k * depth, depth), :], tiles_ref.at[k], sems.at[k]
        )
        for k in range(steps)
    ]
    for copy in copies:
        copy.start()
    size = pieces[0].shape[0]
    sources = [(piece, b) for piece in pieces for b in range(piece.shape[0] // size)]
    for (piece, b), place in zip(sources, places):
        for k in range(steps):
            rows_ref[k, pl.ds(place * size, size), :] = piece[
                pl.ds(b * size, size), pl.ds(k * depth, depth)
            ]
    for now, old in zip((gate_acc, up_acc, squares), before):
        now[...] = old[...]

    for k in range(steps):
        rows = rows_ref[k]
        plain = rows.astype(jnp.float32) * inverse_ref[:, pl.ds(k * depth, depth)]
        square = jnp.broadcast_to(jnp.sum(plain * plain, axis=1, keepdims=True), squares.shape)
        span = pl.ds(row + k * depth, depth)
        gate = jnp.dot(rows, gate_ref[span, :], preferred_element_type=jnp.float32)
        copies[k].wait()
        up = jnp.dot(rows, tiles_ref[k], preferred_element_type=jnp.float32)
        if first and k == 0:
            squares[...], gate_acc[...], up_acc[...] = square, gate, up
        else:
            squares[...] += square
            gate_acc[...] += gate
            up_acc[...] += up

    if last:
        factor = lax.rsqrt(squares[:, :1] / mean_over + 1e-06)
        gate = gate_acc[...] * factor
        hidden_ref[...] = (gate * jax.nn.sigmoid(gate) * (up_acc[...] * factor)).astype(
            jnp.bfloat16
        )


def gather_matmul(
    pieces, places, inverse_gain, gate_proj, up_proj, before, chunk, last, tile=512
):
    columns = pieces[0].shape[1]
    rows = sum(piece.shape[0] for piece in pieces)
    width, units = gate_proj.shape
    steps = columns // tile
    sums = ((rows, units), (rows, units), (rows, 128))
    if last:
        out_shape = jax.ShapeDtypeStruct((rows, units), jnp.bfloat16)
        scratch = [pltpu.VMEM(shape, jnp.float32) for shape in sums]
    else:
        out_shape = tuple(jax.ShapeDtypeStruct(shape, jnp.float32) for shape in sums)
        scratch = []
    vmem = pl.BlockSpec(memory_space=pltpu.VMEM)
    return pl.pallas_call(
        functools.partial(
            gather_matmul_kernel,
            chunk * columns,
            before is None,
            last,
            len(pieces),
            tuple(places),
            width,
        ),
        out_shape=out_shape,
        in_specs=[vmem] * (len(pieces) + 2)
        + [pl.BlockSpec(memory_space=pltpu.HBM)]
        + [vmem] * len(before or ()),
        scratch_shapes=scratch
        + [
            pltpu.VMEM((steps, rows, tile), jnp.bfloat16),
            pltpu.VMEM((steps, tile, units), jnp.bfloat16),
            pltpu.SemaphoreType.DMA((steps,)),
        ],
        compiler_params=pltpu.CompilerParams(vmem_limit_bytes=16 * MIB),
        cost_estimate=pl.CostEstimate(
            flops=4 * rows * columns * units,
            bytes_accessed=4 * columns * units + 2 * rows * columns,
            transcendentals=0,
        ),
        name="gate_up",
    )(*pieces, inverse_gain, in_vmem(gate_proj), in_hbm(up_proj), *(before or ()))


class Grid:
    def __init__(self, count):
        self.count = count
        self.bits = count.bit_length() - 1

    def dims(self, chunk):
        first = [1, 0] if chunk % 2 else [0, 1]
        return first + list(range(2, self.bits))

    def order(self, chunk):
        dims = self.dims(chunk)
        return [
            sum(1 << d for i, d in enumerate(dims) if n >> (self.bits - 1 - i) & 1)
            for n in range(self.count)
        ]

    def places(self, chunk):
        base = self.order(0)
        return [base.index(k) for k in self.order(chunk)]

    def exchange(self, array, k):
        return lax.ppermute(array, "dp", [(i, i ^ k) for i in range(self.count)])

    def exchange_near(self, array):
        half = self.count // 2
        groups = [list(range(half)), list(range(half, self.count))]
        return lax.all_to_all(
            array, "dp", split_axis=0, concat_axis=0, axis_index_groups=groups, tiled=True
        )

    def scatter_sum(self, keep, send, chunk):
        *before, last = self.dims(chunk)
        for d in before:
            keep, send = halve(keep, self.exchange(send, 1 << d))
        return [keep, self.exchange(send, 1 << last)]

    def gather(self, block, chunk):
        pieces = [block]
        for d in reversed(self.dims(chunk)):
            held = jnp.concatenate(pieces, axis=0) if len(pieces) > 1 else block
            pieces.append(self.exchange(held, 1 << d))
        return pieces


def add_up(base, parts):
    for part in parts:
        base = base + part.astype(jnp.float32)
    return base


def body(
    page_pool,
    move_source,
    move_page,
    move_slot,
    row_count,
    lengths,
    page_table,
    queries,
    value_up,
    out_proj,
    residual,
    norm_gain,
    gate_proj,
    up_proj,
    down_proj,
):
    rank_count = lax.axis_size("dp")
    own_rank = lax.axis_index("dp")
    grid = Grid(rank_count)
    rank = own_rank[None]
    move_count = move_page.shape[0] // rank_count
    capacity = max(2, (3 * move_count + 2 * rank_count - 1) // (2 * rank_count))
    slot_count, page_size, feature_width = page_pool.shape
    sources = move_source.T.reshape(rank_count, move_count)
    page_ids = move_page.reshape(rank_count, move_count)
    slot_ids = move_slot.reshape(rank_count, move_count)
    move_order = jnp.arange(move_count)
    earlier = (sources[:, :, None] == sources[:, None, :]) & (
        move_order[None, None, :] < move_order[None, :, None]
    )
    arrival = jnp.sum(earlier.astype(jnp.int32), axis=2)
    split = rank_count // 2
    far_peers = range(split, rank_count)
    pack = functools.partial(pack_pages, page_pool, move_source.T, move_page, rank, rank_count)
    packed = pack(far_peers, False, capacity, rank)
    far_pages = [grid.exchange(pages, k) for k, pages in zip(far_peers, packed)]
    (packed,) = pack(range(split), True, capacity, packed[0])
    near_pages = grid.exchange_near(packed)

    pick = lambda array: lax.dynamic_index_in_dim(array, own_rank, 0, keepdims=False)
    own_slots, own_pages = pick(slot_ids), pick(page_ids)
    peer = pick(sources) ^ own_rank
    place = jnp.where(peer < split, pick(sources) & (split - 1), peer) * capacity + pick(arrival)
    content_of = jnp.where(peer == 0, own_pages, slot_count + place)
    hit = page_table[:, :, None] == own_slots[None, None, :]
    content = jnp.where(
        jnp.any(hit, axis=2), jnp.sum(jnp.where(hit, content_of, 0), axis=2), page_table
    )
    places = slot_count + rank_count * capacity
    counts = slot_counts(content, lengths, jnp.arange(places), page_size)
    far_place = slot_count + split * capacity

    row_slots, head_count = queries.shape[:2]
    by_head_queries = queries.transpose(1, 0, 2).reshape(head_count * row_slots, feature_width)
    state = attend_resident(
        by_head_queries,
        page_pool.reshape(slot_count * page_size, feature_width),
        counts,
        page_size,
    )
    near_pages = near_pages.reshape((split * capacity,) + near_pages.shape[2:])
    state = attend_near(by_head_queries, [near_pages], counts, slot_count, state, page_size)
    far_latents, near_latents = latents(
        by_head_queries,
        far_pages,
        counts,
        far_place,
        state,
        rank,
        row_count,
        page_size,
        rank_count,
        grid.exchange,
    )
    near_latents = grid.exchange_near(near_latents.reshape(split, -1, LATENT))

    width = residual.shape[1]
    columns = width // CHUNKS
    places = [grid.places(c) for c in range(CHUNKS)]
    head_out, *halves = project_first(
        grid.order(0), rank, near_latents, far_latents, value_up, out_proj, columns
    )
    projected = [halves] + [
        project(head_out, out_proj, columns, c, places[c], "project_out") for c in range(1, CHUNKS)
    ]
    middle, gathered = [], []
    for c, (keep, send) in enumerate(projected):
        row_sum, scaled = finish_middle(
            residual, norm_gain[None, :], grid.scatter_sum(keep, send, c), c
        )
        middle.append(row_sum)
        gathered.append(grid.gather(scaled, c))
    inverse_gain = (1.0 / norm_gain)[None, :]
    sums = None
    for c, pieces in enumerate(gathered):
        span = slice(c * columns, (c + 1) * columns)
        sums = gather_matmul(
            pieces,
            places[c],
            inverse_gain[:, span],
            gate_proj,
            up_proj,
            sums,
            c,
            c == CHUNKS - 1,
        )
    hidden = sums
    projected = [
        project(hidden, down_proj, columns, c, places[c], "project_down") for c in range(CHUNKS)
    ]
    outputs = [
        add_up(middle[c], grid.scatter_sum(keep, send, c)).astype(jnp.bfloat16)
        for c, (keep, send) in enumerate(projected)
    ]
    return jnp.concatenate(outputs, axis=1)


def solution(mesh):
    in_specs = (
        P(("rep", "dp"), None, None),
        P("rep", None),
        P("rep"),
        P("rep"),
        P(("rep", "dp")),
        P(("rep", "dp")),
        P(("rep", "dp"), None),
        P(("rep", "dp"), None, None),
        P("dp", None, None),
        P("dp", None),
        P(("rep", "dp"), None),
        P(),
        P(None, "dp"),
        P(None, "dp"),
        P("dp", None),
    )
    out_specs = P(("rep", "dp"), None)
    return jax.shard_map(body, mesh=mesh, in_specs=in_specs, out_specs=out_specs, check_vma=False)
```

```python
import functools
import math

import jax
import jax.numpy as jnp
from jax import lax
from jax.experimental import pallas as pl
from jax.experimental.pallas import tpu as pltpu
from jax.sharding import PartitionSpec as P

LATENT = 512
SOFTMAX_SCALE = 192 ** (-0.5)
LOG2_SCALE = SOFTMAX_SCALE * math.log2(math.e)
MASKED = -1e30
MIB = 1 << 20
CHUNKS = 2
LARGE = pl.CostEstimate(flops=10**11, bytes_accessed=10**8, transcendentals=10**7)


def in_hbm(array):
    return pltpu.with_memory_space_constraint(array, pltpu.HBM)


def in_vmem(array):
    return pltpu.with_memory_space_constraint(array, pltpu.VMEM)


def pack_kernel(peers, near, capacity, moves, source_ref, page_ref, rank_ref, pool_ref, _, *refs):
    out_refs, (pages_ref, sems) = refs[:-2], refs[-2:]
    if near:
        out_refs = [out_refs[0].at[k] for k in range(len(peers))]
    own = rank_ref[0]
    page_size = pages_ref.shape[1]
    half = page_size // 2

    def copy(page, place):
        return pltpu.make_async_copy(pool_ref.at[page], pages_ref.at[place], sems.at[place])

    counts = []
    for k, peer in enumerate(peers):
        first = ((own & ~(len(peers) - 1)) + k if near else own ^ peer) * moves

        def look(i, count, k=k, first=first):
            chosen = (source_ref[0, first + i] == own) & (count < capacity)

            @pl.when(chosen)
            def _():
                copy(page_ref[first + i], k * capacity + count).start()

            return count + chosen.astype(jnp.int32)

        counts.append(lax.fori_loop(0, moves, look, jnp.int32(0)))
    for k in range(len(peers)):
        for c in range(capacity):
            place, out_ref = k * capacity + c, out_refs[k]

            @pl.when(c < counts[k])
            def _(c=c, place=place, out_ref=out_ref):
                copy(0, place).wait()
                for block in range(LATENT // 128):
                    out_ref[c, pl.ds(block * page_size, page_size), :] = pages_ref[
                        place, :, pl.ds(block * 128, 128)
                    ]
                rope = pages_ref[place, :, LATENT:]
                out_ref[c, pl.ds(LATENT // 128 * page_size, half), :] = jnp.concatenate(
                    [rope[:half], rope[half:]], axis=1
                )

            @pl.when(c >= counts[k])
            def _(c=c, out_ref=out_ref):
                out_ref[c] = jnp.zeros(out_ref.shape[1:], out_ref.dtype)


def pack_pages(page_pool, sources, pages, rank, ranks, peers, near, capacity, after):
    page_size, width = page_pool.shape[1:]
    shape = (capacity, page_size * width // 128, 128)
    count = len(peers) * capacity
    shapes = [(len(peers),) + shape] if near else [shape] * len(peers)
    smem = pl.BlockSpec(memory_space=pltpu.SMEM)
    return pl.pallas_call(
        functools.partial(pack_kernel, tuple(peers), near, capacity, pages.shape[0] // ranks),
        out_shape=[jax.ShapeDtypeStruct(shape, page_pool.dtype) for shape in shapes],
        in_specs=[
            smem,
            smem,
            smem,
            pl.BlockSpec(memory_space=pltpu.HBM),
            pl.BlockSpec(memory_space=pl.ANY),
        ],
        out_specs=[pl.BlockSpec(memory_space=pltpu.VMEM)] * len(shapes),
        scratch_shapes=[
            pltpu.VMEM((count, page_size, width), page_pool.dtype),
            pltpu.SemaphoreType.DMA((count,)),
        ],
        compiler_params=pltpu.CompilerParams(vmem_limit_bytes=8 * MIB),
        name="pack_near" if near else "pack_far",
    )(sources, pages, rank, in_hbm(page_pool), after)


def unpack_pages(packed_refs, tokens_ref, page_size):
    half = page_size // 2
    width = tokens_ref.shape[1] - LATENT
    at = 0
    for packed_ref in packed_refs:
        for c in range(packed_ref.shape[0]):
            span = pl.ds(at, page_size)
            for block in range(LATENT // 128):
                tokens_ref[span, pl.ds(block * 128, 128)] = packed_ref[
                    c, pl.ds(block * page_size, page_size), :
                ]
            rope = packed_ref[c, pl.ds(LATENT // 128 * page_size, half), :]
            tokens_ref[span, LATENT:] = jnp.concatenate([rope[:, :width], rope[:, width:]], axis=0)
            at += page_size


def token_bias(counts, first_page, tokens, page_size):
    whole, last, part = counts
    rows, slots = whole.shape
    shift = page_size.bit_length() - 1
    page = (lax.broadcasted_iota(jnp.int32, (slots, tokens), 1) >> shift) + first_page
    spread = jnp.where(
        page == lax.broadcasted_iota(jnp.int32, (slots, tokens), 0), 1.0, 0.0
    ).astype(jnp.bfloat16)
    times = jnp.dot(whole, spread, preferred_element_type=jnp.float32)
    ends = jnp.dot(last, spread, preferred_element_type=jnp.float32)
    offset = lax.broadcasted_iota(jnp.int32, (rows, tokens), 1) & (page_size - 1)
    times = times + jnp.where(offset < part, ends, 0.0)
    return jnp.where(times > 0.5, jnp.log2(jnp.maximum(times, 1.0)), MASKED)


def absorb(raw, tokens, bias, state):
    top, total, acc = state
    rows, count = bias.shape
    scores = (raw.reshape(-1, rows, count) * LOG2_SCALE + bias[None]).reshape(-1, count)
    new_top = jnp.maximum(top, jnp.max(scores, axis=1, keepdims=True))
    weights = jnp.exp2(scores - new_top)
    shrink = jnp.exp2(top - new_top)
    total = total * shrink + jnp.sum(weights, axis=1, keepdims=True)
    acc = acc * shrink + jnp.dot(
        weights.astype(jnp.bfloat16), tokens[:, :LATENT], preferred_element_type=jnp.float32
    )
    return new_top, total, acc


def attend(q_ref, tokens, bias, states):
    size = q_ref.shape[0] // len(states)
    raw = [
        lax.dot_general(
            q_ref[pl.ds(i * size, size), :],
            tokens,
            (((1,), (1,)), ((), ())),
            preferred_element_type=jnp.float32,
        )
        for i in range(len(states))
    ]
    return [absorb(scores, tokens, bias, state) for scores, state in zip(raw, states)]


PARTS = 2


def store_state(states, refs):
    stats_ref, acc_ref = refs
    half = stats_ref.shape[1] // 2
    for i, (top, total, acc) in enumerate(states):
        span = pl.ds(i * acc.shape[0], acc.shape[0])
        stats_ref[span, :] = jnp.concatenate(
            [jnp.broadcast_to(x, (x.shape[0], half)) for x in (top, total)], axis=1
        )
        acc_ref[span, :] = acc


def load_state(refs):
    stats_ref, acc_ref = refs
    half = stats_ref.shape[1] // 2
    size = acc_ref.shape[0] // PARTS
    spans = [pl.ds(i * size, size) for i in range(PARTS)]
    return [
        (stats_ref[span, :1], stats_ref[span, half : half + 1], acc_ref[span, :]) for span in spans
    ]


def counts_of(refs):
    return tuple(ref[...] for ref in refs)


def resident_kernel(
    chunk, page_size, whole_ref, last_ref, part_ref, q_ref, pool_ref, *refs
):
    state_refs, (tokens_ref, bias_ref, sem) = refs[:2], refs[2:]
    token_count = tokens_ref.shape[0]
    count = q_ref.shape[0] // PARTS

    @pl.when(pl.program_id(0) == 0)
    def _():
        copy = pltpu.make_async_copy(pool_ref, tokens_ref, sem)
        copy.start()
        counts = counts_of((whole_ref, last_ref, part_ref))
        for first in range(0, token_count, chunk):
            bias_ref[:, pl.ds(first, chunk)] = token_bias(
                counts, first // page_size, chunk, page_size
            )
        copy.wait()

    def step(index, state):
        span = pl.ds(pl.multiple_of(index * chunk, chunk), chunk)
        return attend(q_ref, tokens_ref[span, :], bias_ref[:, span], state)

    empty = (
        jnp.full((count, 1), MASKED, jnp.float32),
        jnp.zeros((count, 1), jnp.float32),
        jnp.zeros((count, LATENT), jnp.float32),
    )
    states = lax.fori_loop(0, token_count // chunk, step, [empty] * PARTS)
    store_state(states, state_refs)


def state_layout(count, group, block):
    widths = (128, LATENT)
    shapes = tuple(pltpu.HBM((count, w), jnp.float32) for w in widths)
    specs = tuple(pl.BlockSpec((group, w), block) for w in widths)
    return shapes, specs


def attend_resident(queries, pool, counts, page_size, group=512, chunk=1024):
    count, width = queries.shape
    token_count = pool.shape[0]
    rows = counts[0].shape[0]
    block = lambda g: (g, 0)
    fixed = lambda g: (0, 0)
    shapes, specs = state_layout(count, group, block)
    return pl.pallas_call(
        functools.partial(resident_kernel, chunk, page_size),
        out_shape=shapes,
        grid=(count // group,),
        in_specs=[pl.BlockSpec(array.shape, fixed) for array in counts]
        + [pl.BlockSpec((group, width), block), pl.BlockSpec(memory_space=pltpu.HBM)],
        out_specs=specs,
        scratch_shapes=[
            pltpu.VMEM((token_count, width), pool.dtype),
            pltpu.VMEM((rows, token_count), jnp.float32),
            pltpu.SemaphoreType.DMA,
        ],
        compiler_params=pltpu.CompilerParams(vmem_limit_bytes=32 * MIB),
        cost_estimate=LARGE,
        name="attend_resident",
    )(*counts, queries, in_hbm(pool))


def near_kernel(pages, place, page_size, whole_ref, last_ref, part_ref, q_ref, *refs):
    packed_refs, refs = refs[:pages], refs[pages:]
    before, after, (tokens_ref, bias_ref) = refs[:2], refs[2:4], refs[4:]

    @pl.when(pl.program_id(0) == 0)
    def _():
        unpack_pages(packed_refs, tokens_ref, page_size)
        counts = counts_of((whole_ref, last_ref, part_ref))
        bias_ref[...] = token_bias(counts, place, tokens_ref.shape[0], page_size)

    store_state(attend(q_ref, tokens_ref[...], bias_ref[...], load_state(before)), after)


def arrival_operands(packed, counts, fixed):
    once = pl.Buffered(1)
    count_specs = [pl.BlockSpec(array.shape, fixed) for array in counts]
    page_specs = [
        pl.BlockSpec(p.shape, lambda *_: (0, 0, 0), pipeline_mode=once) for p in packed
    ]
    tokens = sum(p.shape[0] for p in packed)
    return count_specs, page_specs, tokens


def attend_near(queries, packed, counts, place, state, page_size, group=512):
    count, width = queries.shape
    block = lambda g: (g, 0)
    count_specs, page_specs, pages = arrival_operands(packed, counts, lambda g: (0, 0))
    tokens = pages * page_size
    shapes, specs = state_layout(count, group, block)
    return pl.pallas_call(
        functools.partial(near_kernel, len(packed), place, page_size),
        out_shape=shapes,
        grid=(count // group,),
        in_specs=count_specs + [pl.BlockSpec((group, width), block)] + page_specs + list(specs),
        out_specs=specs,
        scratch_shapes=[
            pltpu.VMEM((tokens, width), queries.dtype),
            pltpu.VMEM((counts[0].shape[0], tokens), jnp.float32),
        ],
        compiler_params=pltpu.CompilerParams(vmem_limit_bytes=24 * MIB),
        cost_estimate=pl.CostEstimate(
            flops=2 * count * tokens * (width + LATENT),
            bytes_accessed=2 * tokens * width + 8 * count * LATENT,
            transcendentals=count * tokens,
        ),
        name="attend_near",
    )(*counts, queries, *packed, *map(in_hbm, state))


def latents_of(limit_ref, q_ref, tokens, bias, before):
    states = attend(q_ref, tokens, bias, load_state(before))
    latent = jnp.concatenate([acc / total for _, total, acc in states], axis=0)
    latent = latent.reshape(-1, bias.shape[0], LATENT)
    live = lax.broadcasted_iota(jnp.int32, latent.shape, 1) < limit_ref[0]
    return jnp.where(live, latent, 0.0).reshape(-1, LATENT).astype(jnp.bfloat16)


def latents_far_kernel(pages, place, page_size, rank_ref, limit_ref, *refs):
    count_refs, q_ref, refs = refs[:3], refs[3], refs[4:]
    packed_refs, before, refs = refs[:pages], refs[pages : pages + 2], refs[pages + 2 :]
    out_refs, (tokens_ref, bias_ref, latent_ref) = refs[:-3], refs[-3:]
    unpack_pages(packed_refs, tokens_ref, page_size)
    bias_ref[...] = token_bias(counts_of(count_refs), place, tokens_ref.shape[0], page_size)
    latent_ref[...] = latents_of(limit_ref, q_ref, tokens_ref[...], bias_ref[...], before)
    sharing, size = len(out_refs), out_refs[0].shape[0]
    for u, out_ref in enumerate(out_refs):
        at = pl.multiple_of(((rank_ref[0] & (sharing - 1)) ^ u) * size, size)
        out_ref[...] = latent_ref[pl.ds(at, size), :]


def latents_near_kernel(rank_ref, limit_ref, q_ref, tokens_ref, bias_ref, *refs):
    before, out_ref = refs[:2], refs[2]
    out_ref[...] = latents_of(limit_ref, q_ref, tokens_ref[...], bias_ref[...], before)


def latents(queries, packed, counts, place, state, rank, limit, page_size, ranks, exchange):
    count, width = queries.shape
    half, size = ranks // 2, count // ranks
    tokens = sum(p.shape[0] for p in packed) * page_size
    own = lambda g, rank, _: (lax.div(rank[0], half), 0)
    other = lambda g, rank, _: (1 - lax.div(rank[0], half), 0)
    fixed = lambda g, *_: (0, 0)
    state_specs = lambda block: [pl.BlockSpec((count // 2, w), block) for w in (128, LATENT)]
    array = jax.ShapeDtypeStruct
    options = dict(
        compiler_params=pltpu.CompilerParams(vmem_limit_bytes=24 * MIB),
        cost_estimate=pl.CostEstimate(
            flops=count * tokens * (width + LATENT),
            bytes_accessed=2 * tokens * width + 2 * count * LATENT,
            transcendentals=count * tokens // 2,
        ),
    )
    state = [in_hbm(x) for x in state]
    *far, unpacked, bias = pl.pallas_call(
        functools.partial(latents_far_kernel, len(packed), place, page_size),
        out_shape=[array((size, LATENT), jnp.bfloat16)] * half
        + [array((tokens, width), queries.dtype), array((counts[0].shape[0], tokens), jnp.float32)],
        grid_spec=pltpu.PrefetchScalarGridSpec(
            num_scalar_prefetch=2,
            grid=(1,),
            in_specs=[pl.BlockSpec(x.shape, fixed) for x in counts]
            + [pl.BlockSpec((count // 2, width), other)]
            + [pl.BlockSpec(p.shape, lambda *_: (0, 0, 0)) for p in packed]
            + state_specs(other),
            out_specs=[pl.BlockSpec((size, LATENT), fixed)] * half
            + [pl.BlockSpec((tokens, width), fixed)]
            + [pl.BlockSpec((counts[0].shape[0], tokens), fixed)],
            scratch_shapes=[pltpu.VMEM((count // 2, LATENT), jnp.bfloat16)],
        ),
        name="latents_far",
        **options,
    )(rank, limit, *counts, queries, *packed, *state)
    ready = far[0]
    far = [exchange(block, half + u) for u, block in enumerate(far)]
    near = pl.pallas_call(
        latents_near_kernel,
        out_shape=pltpu.HBM((count // 2, LATENT), jnp.bfloat16),
        grid_spec=pltpu.PrefetchScalarGridSpec(
            num_scalar_prefetch=2,
            grid=(1,),
            in_specs=[pl.BlockSpec((count // 2, width), own)]
            + [pl.BlockSpec(x.shape, fixed) for x in (unpacked, bias)]
            + state_specs(own),
            out_specs=pl.BlockSpec((count // 2, LATENT), fixed),
        ),
        name="latents_near",
        **options,
    )(rank, limit, queries, unpacked, bias, *state)
    return far, near, ready


def slot_counts(content, lengths, slots, page_size):
    full = lengths // page_size
    order = jnp.arange(content.shape[1])
    same = content[:, :, None] == slots[None, None, :]
    whole = jnp.sum((same & (order < full[:, None])[:, :, None]).astype(jnp.float32), axis=1)
    last = jnp.sum((same & (order == full[:, None])[:, :, None]).astype(jnp.float32), axis=1)
    return whole.astype(jnp.bfloat16), last.astype(jnp.bfloat16), (lengths % page_size)[:, None]


def multiply_tiles(places, tiles, rows_ref, keep_ref, send_ref):
    half, columns = keep_ref.shape
    size, tile = 2 * half // len(places), columns // len(tiles)
    for n, load in enumerate(tiles):
        product = jnp.dot(rows_ref[...], load(), preferred_element_type=jnp.float32)
        product = product.astype(jnp.bfloat16)
        for to, at in enumerate(places):
            out_ref, to = (keep_ref, to * size) if to * size < half else (send_ref, to * size - half)
            out_ref[pl.ds(to, size), pl.ds(n * tile, tile)] = product[at * size : (at + 1) * size]


def stream(weight_ref, tiles_ref, sems, column):
    width = tiles_ref.shape[2]
    copies = [
        pltpu.make_async_copy(
            weight_ref.at[:, pl.ds(column + n * width, width)], tiles_ref.at[n], sems.at[n]
        )
        for n in range(tiles_ref.shape[0])
    ]
    for copy in copies:
        copy.start()

    def load(n):
        copies[n].wait()
        return tiles_ref[n]

    return [functools.partial(load, n) for n in range(len(copies))]


def preload_kernel(column, _, weight_ref, out_ref, sems):
    count = sems.shape[0]
    width = out_ref.shape[1] // count
    copies = [
        pltpu.make_async_copy(
            weight_ref.at[:, pl.ds(column + n * width, width)],
            out_ref.at[:, pl.ds(n * width, width)],
            sems.at[n],
        )
        for n in range(count)
    ]
    for copy in copies:
        copy.start()
    for copy in copies:
        copy.wait()


def preload(weight, column, columns, after, cost, tile=512):
    shape = (weight.shape[0], columns)
    return pl.pallas_call(
        functools.partial(preload_kernel, column),
        out_shape=pltpu.VMEM(shape, weight.dtype),
        in_specs=[pl.BlockSpec(memory_space=pl.ANY), pl.BlockSpec(memory_space=pltpu.HBM)],
        out_specs=pl.BlockSpec(memory_space=pltpu.VMEM),
        scratch_shapes=[pltpu.SemaphoreType.DMA((columns // tile,))],
        compiler_params=pltpu.CompilerParams(vmem_limit_bytes=2 * MIB),
        cost_estimate=cost,
        name="preload",
    )(after, in_hbm(weight))


def held(weight_ref, tile=512):
    return [
        lambda at=at: weight_ref[:, pl.ds(at, tile)] for at in range(0, weight_ref.shape[1], tile)
    ]


def held_kernel(places, rows_ref, weight_ref, keep_ref, send_ref):
    multiply_tiles(places, held(weight_ref), rows_ref, keep_ref, send_ref)


def project_held(rows, weight, places, name):
    count, depth = rows.shape
    columns = weight.shape[1]
    half = jax.ShapeDtypeStruct((count // 2, columns), jnp.bfloat16)
    return pl.pallas_call(
        functools.partial(held_kernel, tuple(places)),
        out_shape=(half, half),
        compiler_params=pltpu.CompilerParams(vmem_limit_bytes=4 * MIB),
        cost_estimate=pl.CostEstimate(
            flops=2 * count * depth * columns,
            bytes_accessed=2 * count * (columns + depth),
            transcendentals=0,
        ),
        name=name,
    )(rows, in_vmem(weight))


def project_first_kernel(order, rank_ref, near_ref, *refs):
    split = len(order) // 2
    far, refs = refs[:split], refs[split:]
    value_ref, weight_ref, head_ref, keep_ref, send_ref = refs
    heads, width = value_ref.shape[0], value_ref.shape[2]
    own, slots = rank_ref[0] & (split - 1), near_ref.shape[1] // heads
    for h in range(heads):
        span = pl.ds(h * slots, slots)
        rows = jnp.concatenate(
            [near_ref[own ^ k, span, :] if k < split else far[k - split][span, :] for k in order],
            axis=0,
        )
        head_ref[:, pl.ds(h * width, width)] = jnp.dot(
            rows, value_ref[h], preferred_element_type=jnp.float32
        ).astype(jnp.bfloat16)
    multiply_tiles(range(len(order)), held(weight_ref), head_ref, keep_ref, send_ref)


def project_kernel(column, places, rows_ref, weight_ref, keep_ref, send_ref, tiles_ref, sems):
    multiply_tiles(places, stream(weight_ref, tiles_ref, sems, column), rows_ref, keep_ref, send_ref)


def project_options(rows, depth, columns, tile):
    return dict(
        scratch_shapes=[
            pltpu.VMEM((columns // tile, depth, tile), jnp.bfloat16),
            pltpu.SemaphoreType.DMA((columns // tile,)),
        ],
        compiler_params=pltpu.CompilerParams(vmem_limit_bytes=12 * MIB),
        cost_estimate=pl.CostEstimate(
            flops=2 * rows * depth * columns,
            bytes_accessed=2 * depth * columns + 2 * rows * (columns + depth),
            transcendentals=0,
        ),
    )


def project_first(order, rank, near, far, value_up, weight):
    depth, columns = weight.shape
    rows = len(order) * near.shape[1] // value_up.shape[0]
    half = jax.ShapeDtypeStruct((rows // 2, columns), jnp.bfloat16)
    vmem = pl.BlockSpec(memory_space=pltpu.VMEM)
    return pl.pallas_call(
        functools.partial(project_first_kernel, order),
        out_shape=(jax.ShapeDtypeStruct((rows, depth), jnp.bfloat16), half, half),
        in_specs=[pl.BlockSpec(memory_space=pltpu.SMEM)] + [vmem] * (3 + len(far)),
        compiler_params=pltpu.CompilerParams(vmem_limit_bytes=6 * MIB),
        cost_estimate=pl.CostEstimate(
            flops=2 * rows * depth * columns,
            bytes_accessed=2 * rows * (columns + depth),
            transcendentals=0,
        ),
        name="project_first",
    )(rank, near, *far, value_up, in_vmem(weight))


def project(rows, weight, columns, chunk, places, name, tile=512):
    count, depth = rows.shape
    half = jax.ShapeDtypeStruct((count // 2, columns), jnp.bfloat16)
    return pl.pallas_call(
        functools.partial(project_kernel, chunk * columns, tuple(places)),
        out_shape=(half, half),
        in_specs=[pl.BlockSpec(memory_space=pltpu.VMEM), pl.BlockSpec(memory_space=pltpu.HBM)],
        name=name,
        **project_options(count, depth, columns, tile),
    )(rows, in_hbm(weight))


def halve_kernel(keep_ref, came_ref, own_ref, send_ref):
    total = keep_ref[...].astype(jnp.float32) + came_ref[...].astype(jnp.float32)
    half = own_ref.shape[0]
    own_ref[...] = total[:half]
    send_ref[...] = total[half:].astype(send_ref.dtype)


def halve(keep, came):
    shape = (keep.shape[0] // 2, keep.shape[1])
    return pl.pallas_call(
        halve_kernel,
        out_shape=(
            jax.ShapeDtypeStruct(shape, jnp.float32),
            jax.ShapeDtypeStruct(shape, jnp.bfloat16),
        ),
        compiler_params=pltpu.CompilerParams(vmem_limit_bytes=6 * MIB),
        name="halve",
    )(keep, came)


def finish_kernel(residual_ref, gain_ref, own_ref, *refs):
    others, (middle_ref, scaled_ref) = refs[:-2], refs[-2:]
    middle = residual_ref[...].astype(jnp.float32) + own_ref[...]
    for other in others:
        middle = middle + other[...].astype(jnp.float32)
    middle_ref[...] = middle
    scaled_ref[...] = (middle * gain_ref[...]).astype(scaled_ref.dtype)


def finish_middle(residual, gain, sums, chunk):
    rows, columns = sums[0].shape
    here = lambda _: (0, chunk)
    block = pl.BlockSpec((rows, columns), lambda _: (0, 0))
    return pl.pallas_call(
        finish_kernel,
        out_shape=(
            jax.ShapeDtypeStruct((rows, columns), jnp.float32),
            jax.ShapeDtypeStruct((rows, columns), jnp.bfloat16),
        ),
        grid=(1,),
        in_specs=[pl.BlockSpec((rows, columns), here), pl.BlockSpec((1, columns), here)]
        + [block] * len(sums),
        out_specs=(block, block),
        compiler_params=pltpu.CompilerParams(vmem_limit_bytes=4 * MIB),
        name="finish_middle",
    )(residual, gain, *sums)


def gather_matmul_kernel(row, first, last, n_pieces, places, mean_over, *refs):
    pieces, refs = refs[:n_pieces], refs[n_pieces:]
    inverse_ref, gate_ref, up_ref, refs = refs[0], refs[1], refs[2], refs[3:]
    before, refs = ((), refs[1:]) if first else (refs[:3], refs[4:])
    if last:
        hidden_ref, gate_acc, up_acc, squares, *refs = refs
    else:
        gate_acc, up_acc, squares, *refs = refs
    rows_ref, tiles_ref, sems = refs
    steps, _, depth = rows_ref.shape
    copies = [
        pltpu.make_async_copy(
            up_ref.at[pl.ds(row + k * depth, depth), :], tiles_ref.at[k], sems.at[k]
        )
        for k in range(steps)
    ]
    for copy in copies:
        copy.start()
    size = pieces[0].shape[0]
    sources = [(piece, b) for piece in pieces for b in range(piece.shape[0] // size)]
    for (piece, b), place in zip(sources, places):
        for k in range(steps):
            rows_ref[k, pl.ds(place * size, size), :] = piece[
                pl.ds(b * size, size), pl.ds(k * depth, depth)
            ]
    for now, old in zip((gate_acc, up_acc, squares), before):
        now[...] = old[...]

    for k in range(steps):
        rows = rows_ref[k]
        plain = rows.astype(jnp.float32) * inverse_ref[:, pl.ds(k * depth, depth)]
        square = jnp.broadcast_to(jnp.sum(plain * plain, axis=1, keepdims=True), squares.shape)
        span = pl.ds(row + k * depth, depth)
        gate = jnp.dot(rows, gate_ref[span, :], preferred_element_type=jnp.float32)
        copies[k].wait()
        up = jnp.dot(rows, tiles_ref[k], preferred_element_type=jnp.float32)
        if first and k == 0:
            squares[...], gate_acc[...], up_acc[...] = square, gate, up
        else:
            squares[...] += square
            gate_acc[...] += gate
            up_acc[...] += up

    if last:
        factor = lax.rsqrt(squares[:, :1] / mean_over + 1e-06)
        gate = gate_acc[...] * factor
        hidden_ref[...] = (gate * jax.nn.sigmoid(gate) * (up_acc[...] * factor)).astype(
            jnp.bfloat16
        )


def gather_matmul(
    pieces, places, inverse_gain, gate_proj, up_proj, before, chunk, last, after, tile=512
):
    columns = pieces[0].shape[1]
    rows = sum(piece.shape[0] for piece in pieces)
    width, units = gate_proj.shape
    steps = columns // tile
    sums = ((rows, units), (rows, units), (rows, 128))
    if last:
        out_shape = jax.ShapeDtypeStruct((rows, units), jnp.bfloat16)
        scratch = [pltpu.VMEM(shape, jnp.float32) for shape in sums]
    else:
        out_shape = tuple(jax.ShapeDtypeStruct(shape, jnp.float32) for shape in sums)
        scratch = []
    vmem = pl.BlockSpec(memory_space=pltpu.VMEM)
    return pl.pallas_call(
        functools.partial(
            gather_matmul_kernel,
            chunk * columns,
            before is None,
            last,
            len(pieces),
            tuple(places),
            width,
        ),
        out_shape=out_shape,
        in_specs=[vmem] * (len(pieces) + 2)
        + [pl.BlockSpec(memory_space=pltpu.HBM)]
        + [vmem] * len(before or ())
        + [pl.BlockSpec(memory_space=pl.ANY)],
        scratch_shapes=scratch
        + [
            pltpu.VMEM((steps, rows, tile), jnp.bfloat16),
            pltpu.VMEM((steps, tile, units), jnp.bfloat16),
            pltpu.SemaphoreType.DMA((steps,)),
        ],
        compiler_params=pltpu.CompilerParams(vmem_limit_bytes=12 * MIB),
        cost_estimate=pl.CostEstimate(
            flops=4 * rows * columns * units,
            bytes_accessed=4 * columns * units + 2 * rows * columns,
            transcendentals=0,
        ),
        name="gate_up",
    )(*pieces, inverse_gain, in_vmem(gate_proj), in_hbm(up_proj), *(before or ()), after)


class Grid:
    def __init__(self, count):
        self.count = count
        self.bits = count.bit_length() - 1

    def dims(self, chunk):
        first = [1, 0] if chunk % 2 else [0, 1]
        return first + list(range(2, self.bits))

    def order(self, chunk):
        dims = self.dims(chunk)
        return [
            sum(1 << d for i, d in enumerate(dims) if n >> (self.bits - 1 - i) & 1)
            for n in range(self.count)
        ]

    def places(self, chunk):
        base = self.order(0)
        return [base.index(k) for k in self.order(chunk)]

    def exchange(self, array, k):
        return lax.ppermute(array, "dp", [(i, i ^ k) for i in range(self.count)])

    def exchange_near(self, array):
        half = self.count // 2
        groups = [list(range(half)), list(range(half, self.count))]
        return lax.all_to_all(
            array, "dp", split_axis=0, concat_axis=0, axis_index_groups=groups, tiled=True
        )

    def scatter_sum(self, keep, send, chunk):
        *before, last = self.dims(chunk)
        for d in before:
            keep, send = halve(keep, self.exchange(send, 1 << d))
        return [keep, self.exchange(send, 1 << last)]

    def gather(self, block, chunk):
        pieces = [block]
        for d in reversed(self.dims(chunk)):
            held = jnp.concatenate(pieces, axis=0) if len(pieces) > 1 else block
            pieces.append(self.exchange(held, 1 << d))
        return pieces


def add_up(base, parts):
    for part in parts:
        base = base + part.astype(jnp.float32)
    return base


def body(
    page_pool,
    move_source,
    move_page,
    move_slot,
    row_count,
    lengths,
    page_table,
    queries,
    value_up,
    out_proj,
    residual,
    norm_gain,
    gate_proj,
    up_proj,
    down_proj,
):
    rank_count = lax.axis_size("dp")
    own_rank = lax.axis_index("dp")
    grid = Grid(rank_count)
    rank = own_rank[None]
    move_count = move_page.shape[0] // rank_count
    capacity = max(2, (3 * move_count + 2 * rank_count - 1) // (2 * rank_count))
    slot_count, page_size, feature_width = page_pool.shape
    sources = move_source.T.reshape(rank_count, move_count)
    page_ids = move_page.reshape(rank_count, move_count)
    slot_ids = move_slot.reshape(rank_count, move_count)
    move_order = jnp.arange(move_count)
    earlier = (sources[:, :, None] == sources[:, None, :]) & (
        move_order[None, None, :] < move_order[None, :, None]
    )
    arrival = jnp.sum(earlier.astype(jnp.int32), axis=2)
    split = rank_count // 2
    far_peers = range(split, rank_count)
    pack = functools.partial(pack_pages, page_pool, move_source.T, move_page, rank, rank_count)
    packed = pack(far_peers, False, capacity, rank)
    far_pages = [grid.exchange(pages, k) for k, pages in zip(far_peers, packed)]
    (packed,) = pack(range(split), True, capacity, packed[0])
    near_pages = grid.exchange_near(packed)

    pick = lambda array: lax.dynamic_index_in_dim(array, own_rank, 0, keepdims=False)
    own_slots, own_pages = pick(slot_ids), pick(page_ids)
    peer = pick(sources) ^ own_rank
    place = jnp.where(peer < split, pick(sources) & (split - 1), peer) * capacity + pick(arrival)
    content_of = jnp.where(peer == 0, own_pages, slot_count + place)
    hit = page_table[:, :, None] == own_slots[None, None, :]
    content = jnp.where(
        jnp.any(hit, axis=2), jnp.sum(jnp.where(hit, content_of, 0), axis=2), page_table
    )
    places = slot_count + rank_count * capacity
    counts = slot_counts(content, lengths, jnp.arange(places), page_size)
    far_place = slot_count + split * capacity

    row_slots, head_count = queries.shape[:2]
    by_head_queries = queries.transpose(1, 0, 2).reshape(head_count * row_slots, feature_width)
    state = attend_resident(
        by_head_queries,
        page_pool.reshape(slot_count * page_size, feature_width),
        counts,
        page_size,
    )
    near_pages = near_pages.reshape((split * capacity,) + near_pages.shape[2:])
    state = attend_near(by_head_queries, [near_pages], counts, slot_count, state, page_size)
    far_latents, near_latents, ready = latents(
        by_head_queries,
        far_pages,
        counts,
        far_place,
        state,
        rank,
        row_count,
        page_size,
        rank_count,
        grid.exchange,
    )
    near_latents = grid.exchange_near(near_latents.reshape(split, -1, LATENT))

    width = residual.shape[1]
    columns = width // CHUNKS
    places = [grid.places(c) for c in range(CHUNKS)]
    out_first = preload(out_proj, 0, columns, ready, LARGE)
    head_out, *halves = project_first(
        grid.order(0), rank, near_latents, far_latents, value_up, out_first
    )
    projected = [halves] + [
        project(head_out, out_proj, columns, c, places[c], "project_out") for c in range(1, CHUNKS)
    ]
    middle, gathered = [], []
    for c, (keep, send) in enumerate(projected):
        row_sum, scaled = finish_middle(
            residual, norm_gain[None, :], grid.scatter_sum(keep, send, c), c
        )
        middle.append(row_sum)
        gathered.append(grid.gather(scaled, c))
    down_first = preload(
        down_proj,
        0,
        columns,
        gathered[-1][0],
        pl.CostEstimate(
            flops=0, bytes_accessed=2 * down_proj.shape[0] * columns, transcendentals=0
        ),
    )
    inverse_gain = (1.0 / norm_gain)[None, :]
    sums = None
    for c, pieces in enumerate(gathered):
        span = slice(c * columns, (c + 1) * columns)
        sums = gather_matmul(
            pieces,
            places[c],
            inverse_gain[:, span],
            gate_proj,
            up_proj,
            sums,
            c,
            c == CHUNKS - 1,
            down_first,
        )
    hidden = sums
    projected = [project_held(hidden, down_first, places[0], "project_down")] + [
        project(hidden, down_proj, columns, c, places[c], "project_down") for c in range(1, CHUNKS)
    ]
    outputs = [
        add_up(middle[c], grid.scatter_sum(keep, send, c)).astype(jnp.bfloat16)
        for c, (keep, send) in enumerate(projected)
    ]
    return jnp.concatenate(outputs, axis=1)


def solution(mesh):
    in_specs = (
        P(("rep", "dp"), None, None),
        P("rep", None),
        P("rep"),
        P("rep"),
        P(("rep", "dp")),
        P(("rep", "dp")),
        P(("rep", "dp"), None),
        P(("rep", "dp"), None, None),
        P("dp", None, None),
        P("dp", None),
        P(("rep", "dp"), None),
        P(),
        P(None, "dp"),
        P(None, "dp"),
        P("dp", None),
    )
    out_specs = P(("rep", "dp"), None)
    return jax.shard_map(body, mesh=mesh, in_specs=in_specs, out_specs=out_specs, check_vma=False)
```

```python
import functools
import math

import jax
import jax.numpy as jnp
from jax import lax
from jax.experimental import pallas as pl
from jax.experimental.pallas import tpu as pltpu
from jax.sharding import PartitionSpec as P

LATENT = 512
SOFTMAX_SCALE = 192 ** (-0.5)
LOG2_SCALE = SOFTMAX_SCALE * math.log2(math.e)
MASKED = -1e30
MIB = 1 << 20
CHUNKS = 2
LARGE = pl.CostEstimate(flops=10**11, bytes_accessed=10**8, transcendentals=10**7)


def in_hbm(array):
    return pltpu.with_memory_space_constraint(array, pltpu.HBM)


def in_vmem(array):
    return pltpu.with_memory_space_constraint(array, pltpu.VMEM)


def pack_kernel(peers, near, capacity, moves, source_ref, page_ref, rank_ref, pool_ref, _, *refs):
    out_refs, (pages_ref, sems) = refs[:-2], refs[-2:]
    if near:
        out_refs = [out_refs[0].at[k] for k in range(len(peers))]
    own = rank_ref[0]
    page_size = pages_ref.shape[1]
    half = page_size // 2

    def copy(page, place):
        return pltpu.make_async_copy(pool_ref.at[page], pages_ref.at[place], sems.at[place])

    counts = []
    for k, peer in enumerate(peers):
        first = ((own & ~(len(peers) - 1)) + k if near else own ^ peer) * moves

        def look(i, count, k=k, first=first):
            chosen = (source_ref[0, first + i] == own) & (count < capacity)

            @pl.when(chosen)
            def _():
                copy(page_ref[first + i], k * capacity + count).start()

            return count + chosen.astype(jnp.int32)

        counts.append(lax.fori_loop(0, moves, look, jnp.int32(0)))
    for k in range(len(peers)):
        for c in range(capacity):
            place, out_ref = k * capacity + c, out_refs[k]

            @pl.when(c < counts[k])
            def _(c=c, place=place, out_ref=out_ref):
                copy(0, place).wait()
                for block in range(LATENT // 128):
                    out_ref[c, pl.ds(block * page_size, page_size), :] = pages_ref[
                        place, :, pl.ds(block * 128, 128)
                    ]
                rope = pages_ref[place, :, LATENT:]
                out_ref[c, pl.ds(LATENT // 128 * page_size, half), :] = jnp.concatenate(
                    [rope[:half], rope[half:]], axis=1
                )

            @pl.when(c >= counts[k])
            def _(c=c, out_ref=out_ref):
                out_ref[c] = jnp.zeros(out_ref.shape[1:], out_ref.dtype)


def pack_pages(page_pool, sources, pages, rank, ranks, peers, near, capacity, after):
    page_size, width = page_pool.shape[1:]
    shape = (capacity, page_size * width // 128, 128)
    count = len(peers) * capacity
    shapes = [(len(peers),) + shape] if near else [shape] * len(peers)
    smem = pl.BlockSpec(memory_space=pltpu.SMEM)
    return pl.pallas_call(
        functools.partial(pack_kernel, tuple(peers), near, capacity, pages.shape[0] // ranks),
        out_shape=[jax.ShapeDtypeStruct(shape, page_pool.dtype) for shape in shapes],
        in_specs=[
            smem,
            smem,
            smem,
            pl.BlockSpec(memory_space=pltpu.HBM),
            pl.BlockSpec(memory_space=pl.ANY),
        ],
        out_specs=[pl.BlockSpec(memory_space=pltpu.VMEM)] * len(shapes),
        scratch_shapes=[
            pltpu.VMEM((count, page_size, width), page_pool.dtype),
            pltpu.SemaphoreType.DMA((count,)),
        ],
        compiler_params=pltpu.CompilerParams(vmem_limit_bytes=8 * MIB),
        name="pack_near" if near else "pack_far",
    )(sources, pages, rank, in_hbm(page_pool), after)


def unpack_pages(packed_refs, tokens_ref, page_size):
    half = page_size // 2
    width = tokens_ref.shape[1] - LATENT
    at = 0
    for packed_ref in packed_refs:
        for c in range(packed_ref.shape[0]):
            span = pl.ds(at, page_size)
            for block in range(LATENT // 128):
                tokens_ref[span, pl.ds(block * 128, 128)] = packed_ref[
                    c, pl.ds(block * page_size, page_size), :
                ]
            rope = packed_ref[c, pl.ds(LATENT // 128 * page_size, half), :]
            tokens_ref[span, LATENT:] = jnp.concatenate([rope[:, :width], rope[:, width:]], axis=0)
            at += page_size


def token_bias(counts, first_page, tokens, page_size):
    whole, last, part = counts
    rows, slots = whole.shape
    shift = page_size.bit_length() - 1
    page = (lax.broadcasted_iota(jnp.int32, (slots, tokens), 1) >> shift) + first_page
    spread = jnp.where(
        page == lax.broadcasted_iota(jnp.int32, (slots, tokens), 0), 1.0, 0.0
    ).astype(jnp.bfloat16)
    times = jnp.dot(whole, spread, preferred_element_type=jnp.float32)
    ends = jnp.dot(last, spread, preferred_element_type=jnp.float32)
    offset = lax.broadcasted_iota(jnp.int32, (rows, tokens), 1) & (page_size - 1)
    times = times + jnp.where(offset < part, ends, 0.0)
    return jnp.where(times > 0.5, jnp.log2(jnp.maximum(times, 1.0)), MASKED)


def absorb(raw, tokens, bias, state):
    top, total, acc = state
    rows, count = bias.shape
    scores = (raw.reshape(-1, rows, count) * LOG2_SCALE + bias[None]).reshape(-1, count)
    new_top = jnp.maximum(top, jnp.max(scores, axis=1, keepdims=True))
    weights = jnp.exp2(scores - new_top)
    shrink = jnp.exp2(top - new_top)
    total = total * shrink + jnp.sum(weights, axis=1, keepdims=True)
    acc = acc * shrink + jnp.dot(
        weights.astype(jnp.bfloat16), tokens[:, :LATENT], preferred_element_type=jnp.float32
    )
    return new_top, total, acc


def attend(q_ref, tokens, bias, states):
    size = q_ref.shape[0] // len(states)
    raw = [
        lax.dot_general(
            q_ref[pl.ds(i * size, size), :],
            tokens,
            (((1,), (1,)), ((), ())),
            preferred_element_type=jnp.float32,
        )
        for i in range(len(states))
    ]
    return [absorb(scores, tokens, bias, state) for scores, state in zip(raw, states)]


PARTS = 2


def store_state(states, refs):
    stats_ref, acc_ref = refs
    half = stats_ref.shape[1] // 2
    for i, (top, total, acc) in enumerate(states):
        span = pl.ds(i * acc.shape[0], acc.shape[0])
        stats_ref[span, :] = jnp.concatenate(
            [jnp.broadcast_to(x, (x.shape[0], half)) for x in (top, total)], axis=1
        )
        acc_ref[span, :] = acc


def load_state(refs):
    stats_ref, acc_ref = refs
    half = stats_ref.shape[1] // 2
    size = acc_ref.shape[0] // PARTS
    spans = [pl.ds(i * size, size) for i in range(PARTS)]
    return [
        (stats_ref[span, :1], stats_ref[span, half : half + 1], acc_ref[span, :]) for span in spans
    ]


def counts_of(refs):
    return tuple(ref[...] for ref in refs)


def resident_kernel(
    chunk, page_size, whole_ref, last_ref, part_ref, q_ref, pool_ref, *refs
):
    state_refs, (tokens_ref, bias_ref, sem) = refs[:2], refs[2:]
    token_count = tokens_ref.shape[0]
    count = q_ref.shape[0] // PARTS

    @pl.when(pl.program_id(0) == 0)
    def _():
        copy = pltpu.make_async_copy(pool_ref, tokens_ref, sem)
        copy.start()
        counts = counts_of((whole_ref, last_ref, part_ref))
        for first in range(0, token_count, chunk):
            bias_ref[:, pl.ds(first, chunk)] = token_bias(
                counts, first // page_size, chunk, page_size
            )
        copy.wait()

    def step(index, state):
        span = pl.ds(pl.multiple_of(index * chunk, chunk), chunk)
        return attend(q_ref, tokens_ref[span, :], bias_ref[:, span], state)

    empty = (
        jnp.full((count, 1), MASKED, jnp.float32),
        jnp.zeros((count, 1), jnp.float32),
        jnp.zeros((count, LATENT), jnp.float32),
    )
    states = lax.fori_loop(0, token_count // chunk, step, [empty] * PARTS)
    store_state(states, state_refs)


def state_layout(count, group, block):
    widths = (128, LATENT)
    shapes = tuple(pltpu.HBM((count, w), jnp.float32) for w in widths)
    specs = tuple(pl.BlockSpec((group, w), block) for w in widths)
    return shapes, specs


def attend_resident(queries, pool, counts, page_size, group=512, chunk=1024):
    count, width = queries.shape
    token_count = pool.shape[0]
    rows = counts[0].shape[0]
    block = lambda g: (g, 0)
    fixed = lambda g: (0, 0)
    shapes, specs = state_layout(count, group, block)
    return pl.pallas_call(
        functools.partial(resident_kernel, chunk, page_size),
        out_shape=shapes,
        grid=(count // group,),
        in_specs=[pl.BlockSpec(array.shape, fixed) for array in counts]
        + [pl.BlockSpec((group, width), block), pl.BlockSpec(memory_space=pltpu.HBM)],
        out_specs=specs,
        scratch_shapes=[
            pltpu.VMEM((token_count, width), pool.dtype),
            pltpu.VMEM((rows, token_count), jnp.float32),
            pltpu.SemaphoreType.DMA,
        ],
        compiler_params=pltpu.CompilerParams(vmem_limit_bytes=32 * MIB),
        cost_estimate=LARGE,
        name="attend_resident",
    )(*counts, queries, in_hbm(pool))


def near_kernel(pages, place, page_size, whole_ref, last_ref, part_ref, q_ref, *refs):
    packed_refs, refs = refs[:pages], refs[pages:]
    before, after, (tokens_ref, bias_ref) = refs[:2], refs[2:4], refs[4:]

    @pl.when(pl.program_id(0) == 0)
    def _():
        unpack_pages(packed_refs, tokens_ref, page_size)
        counts = counts_of((whole_ref, last_ref, part_ref))
        bias_ref[...] = token_bias(counts, place, tokens_ref.shape[0], page_size)

    store_state(attend(q_ref, tokens_ref[...], bias_ref[...], load_state(before)), after)


def arrival_operands(packed, counts, fixed):
    once = pl.Buffered(1)
    count_specs = [pl.BlockSpec(array.shape, fixed) for array in counts]
    page_specs = [
        pl.BlockSpec(p.shape, lambda *_: (0, 0, 0), pipeline_mode=once) for p in packed
    ]
    tokens = sum(p.shape[0] for p in packed)
    return count_specs, page_specs, tokens


def attend_near(queries, packed, counts, place, state, page_size, group=512):
    count, width = queries.shape
    block = lambda g: (g, 0)
    count_specs, page_specs, pages = arrival_operands(packed, counts, lambda g: (0, 0))
    tokens = pages * page_size
    shapes, specs = state_layout(count, group, block)
    return pl.pallas_call(
        functools.partial(near_kernel, len(packed), place, page_size),
        out_shape=shapes,
        grid=(count // group,),
        in_specs=count_specs + [pl.BlockSpec((group, width), block)] + page_specs + list(specs),
        out_specs=specs,
        scratch_shapes=[
            pltpu.VMEM((tokens, width), queries.dtype),
            pltpu.VMEM((counts[0].shape[0], tokens), jnp.float32),
        ],
        compiler_params=pltpu.CompilerParams(vmem_limit_bytes=24 * MIB),
        cost_estimate=pl.CostEstimate(
            flops=2 * count * tokens * (width + LATENT),
            bytes_accessed=2 * tokens * width + 8 * count * LATENT,
            transcendentals=count * tokens,
        ),
        name="attend_near",
    )(*counts, queries, *packed, *map(in_hbm, state))


def latents_of(limit_ref, q_ref, tokens, bias, before):
    states = attend(q_ref, tokens, bias, load_state(before))
    latent = jnp.concatenate([acc / total for _, total, acc in states], axis=0)
    latent = latent.reshape(-1, bias.shape[0], LATENT)
    live = lax.broadcasted_iota(jnp.int32, latent.shape, 1) < limit_ref[0]
    return jnp.where(live, latent, 0.0).reshape(-1, LATENT).astype(jnp.bfloat16)


def latents_far_kernel(pages, place, page_size, rank_ref, limit_ref, *refs):
    count_refs, q_ref, refs = refs[:3], refs[3], refs[4:]
    packed_refs, before, refs = refs[:pages], refs[pages : pages + 2], refs[pages + 2 :]
    out_refs, (tokens_ref, bias_ref, latent_ref) = refs[:-3], refs[-3:]
    unpack_pages(packed_refs, tokens_ref, page_size)
    bias_ref[...] = token_bias(counts_of(count_refs), place, tokens_ref.shape[0], page_size)
    latent_ref[...] = latents_of(limit_ref, q_ref, tokens_ref[...], bias_ref[...], before)
    sharing, size = len(out_refs), out_refs[0].shape[0]
    for u, out_ref in enumerate(out_refs):
        at = pl.multiple_of(((rank_ref[0] & (sharing - 1)) ^ u) * size, size)
        out_ref[...] = latent_ref[pl.ds(at, size), :]


def latents_near_kernel(rank_ref, limit_ref, q_ref, tokens_ref, bias_ref, *refs):
    before, out_ref = refs[:2], refs[2]
    out_ref[...] = latents_of(limit_ref, q_ref, tokens_ref[...], bias_ref[...], before)


def latents(queries, packed, counts, place, state, rank, limit, page_size, ranks, exchange):
    count, width = queries.shape
    half, size = ranks // 2, count // ranks
    tokens = sum(p.shape[0] for p in packed) * page_size
    own = lambda g, rank, _: (lax.div(rank[0], half), 0)
    other = lambda g, rank, _: (1 - lax.div(rank[0], half), 0)
    fixed = lambda g, *_: (0, 0)
    state_specs = lambda block: [pl.BlockSpec((count // 2, w), block) for w in (128, LATENT)]
    array = jax.ShapeDtypeStruct
    options = dict(
        compiler_params=pltpu.CompilerParams(vmem_limit_bytes=24 * MIB),
        cost_estimate=pl.CostEstimate(
            flops=count * tokens * (width + LATENT),
            bytes_accessed=2 * tokens * width + 2 * count * LATENT,
            transcendentals=count * tokens // 2,
        ),
    )
    state = [in_hbm(x) for x in state]
    *far, unpacked, bias = pl.pallas_call(
        functools.partial(latents_far_kernel, len(packed), place, page_size),
        out_shape=[array((size, LATENT), jnp.bfloat16)] * half
        + [array((tokens, width), queries.dtype), array((counts[0].shape[0], tokens), jnp.float32)],
        grid_spec=pltpu.PrefetchScalarGridSpec(
            num_scalar_prefetch=2,
            grid=(1,),
            in_specs=[pl.BlockSpec(x.shape, fixed) for x in counts]
            + [pl.BlockSpec((count // 2, width), other)]
            + [pl.BlockSpec(p.shape, lambda *_: (0, 0, 0)) for p in packed]
            + state_specs(other),
            out_specs=[pl.BlockSpec((size, LATENT), fixed)] * half
            + [pl.BlockSpec((tokens, width), fixed)]
            + [pl.BlockSpec((counts[0].shape[0], tokens), fixed)],
            scratch_shapes=[pltpu.VMEM((count // 2, LATENT), jnp.bfloat16)],
        ),
        name="latents_far",
        **options,
    )(rank, limit, *counts, queries, *packed, *state)
    ready = far[0]
    far = [exchange(block, half + u) for u, block in enumerate(far)]
    near = pl.pallas_call(
        latents_near_kernel,
        out_shape=pltpu.HBM((count // 2, LATENT), jnp.bfloat16),
        grid_spec=pltpu.PrefetchScalarGridSpec(
            num_scalar_prefetch=2,
            grid=(1,),
            in_specs=[pl.BlockSpec((count // 2, width), own)]
            + [pl.BlockSpec(x.shape, fixed) for x in (unpacked, bias)]
            + state_specs(own),
            out_specs=pl.BlockSpec((count // 2, LATENT), fixed),
        ),
        name="latents_near",
        **options,
    )(rank, limit, queries, unpacked, bias, *state)
    return far, near, ready


def slot_counts(content, lengths, slots, page_size):
    full = lengths // page_size
    order = jnp.arange(content.shape[1])
    same = content[:, :, None] == slots[None, None, :]
    whole = jnp.sum((same & (order < full[:, None])[:, :, None]).astype(jnp.float32), axis=1)
    last = jnp.sum((same & (order == full[:, None])[:, :, None]).astype(jnp.float32), axis=1)
    return whole.astype(jnp.bfloat16), last.astype(jnp.bfloat16), (lengths % page_size)[:, None]


def multiply_tiles(places, tiles, rows_ref, keep_ref, send_ref):
    half, columns = keep_ref.shape
    size, tile = 2 * half // len(places), columns // len(tiles)
    for n, load in enumerate(tiles):
        product = jnp.dot(rows_ref[...], load(), preferred_element_type=jnp.float32)
        product = product.astype(jnp.bfloat16)
        for to, at in enumerate(places):
            out_ref, to = (keep_ref, to * size) if to * size < half else (send_ref, to * size - half)
            out_ref[pl.ds(to, size), pl.ds(n * tile, tile)] = product[at * size : (at + 1) * size]


def stream(weight_ref, tiles_ref, sems, column):
    width = tiles_ref.shape[2]
    copies = [
        pltpu.make_async_copy(
            weight_ref.at[:, pl.ds(column + n * width, width)], tiles_ref.at[n], sems.at[n]
        )
        for n in range(tiles_ref.shape[0])
    ]
    for copy in copies:
        copy.start()

    def load(n):
        copies[n].wait()
        return tiles_ref[n]

    return [functools.partial(load, n) for n in range(len(copies))]


def preload_kernel(column, _, weight_ref, out_ref, sems):
    count = sems.shape[0]
    width = out_ref.shape[1] // count
    copies = [
        pltpu.make_async_copy(
            weight_ref.at[:, pl.ds(column + n * width, width)],
            out_ref.at[:, pl.ds(n * width, width)],
            sems.at[n],
        )
        for n in range(count)
    ]
    for copy in copies:
        copy.start()
    for copy in copies:
        copy.wait()


def preload(weight, column, columns, after, cost, tile=512):
    shape = (weight.shape[0], columns)
    return pl.pallas_call(
        functools.partial(preload_kernel, column),
        out_shape=pltpu.VMEM(shape, weight.dtype),
        in_specs=[pl.BlockSpec(memory_space=pl.ANY), pl.BlockSpec(memory_space=pltpu.HBM)],
        out_specs=pl.BlockSpec(memory_space=pltpu.VMEM),
        scratch_shapes=[pltpu.SemaphoreType.DMA((columns // tile,))],
        compiler_params=pltpu.CompilerParams(vmem_limit_bytes=2 * MIB),
        cost_estimate=cost,
        name="preload",
    )(after, in_hbm(weight))


def held(weight_ref, tile=512):
    return [
        lambda at=at: weight_ref[:, pl.ds(at, tile)] for at in range(0, weight_ref.shape[1], tile)
    ]


def held_kernel(places, rows_ref, weight_ref, keep_ref, send_ref):
    multiply_tiles(places, held(weight_ref), rows_ref, keep_ref, send_ref)


def project_held(rows, weight, places, name):
    count, depth = rows.shape
    columns = weight.shape[1]
    half = jax.ShapeDtypeStruct((count // 2, columns), jnp.bfloat16)
    return pl.pallas_call(
        functools.partial(held_kernel, tuple(places)),
        out_shape=(half, half),
        compiler_params=pltpu.CompilerParams(vmem_limit_bytes=4 * MIB),
        cost_estimate=pl.CostEstimate(
            flops=2 * count * depth * columns,
            bytes_accessed=2 * count * (columns + depth),
            transcendentals=0,
        ),
        name=name,
    )(rows, in_vmem(weight))


def head_values(parts, value_ref, slots, out):
    heads = value_ref.shape[0] // LATENT
    for h in range(heads):
        rows = jnp.concatenate([part(pl.ds(h * slots, slots)) for part in parts], axis=0)
        values = value_ref[pl.ds(h * LATENT, LATENT), :]
        out(h, jnp.dot(rows, values, preferred_element_type=jnp.float32).astype(jnp.bfloat16))


def value_near_kernel(rank_ref, near_ref, value_ref, out_ref):
    split, width = near_ref.shape[0], value_ref.shape[1]
    own, slots = rank_ref[0] & (split - 1), near_ref.shape[1] * LATENT // value_ref.shape[0]
    parts = [lambda span, k=k: near_ref[own ^ k, span, :] for k in range(split)]

    def out(h, rows):
        out_ref[:, pl.ds(h * width, width)] = rows

    head_values(parts, value_ref, slots, out)


def value_near(rank, near, values):
    heads = values.shape[0] // LATENT
    shape = (near.shape[0] * near.shape[1] // heads, heads * values.shape[1])
    vmem = pl.BlockSpec(memory_space=pltpu.VMEM)
    return pl.pallas_call(
        value_near_kernel,
        out_shape=jax.ShapeDtypeStruct(shape, jnp.bfloat16),
        in_specs=[pl.BlockSpec(memory_space=pltpu.SMEM), vmem, vmem],
        compiler_params=pltpu.CompilerParams(vmem_limit_bytes=4 * MIB),
        name="value_near",
    )(rank, near, values)


def project_first_kernel(order, near_ref, *refs):
    split = len(order) // 2
    far, refs = refs[:split], refs[split:]
    value_ref, weight_ref, head_ref, keep_ref, send_ref, tiles_ref, sems = refs
    tiles = stream(weight_ref, tiles_ref, sems, 0)
    slots, width = near_ref.shape[0] // split, value_ref.shape[1]
    place = {k: pl.ds(n * slots, slots) for n, k in enumerate(order)}
    for k in range(split):
        head_ref[place[k], :] = near_ref[pl.ds(k * slots, slots), :]

    def out(h, rows):
        for k in range(split):
            head_ref[place[split + k], pl.ds(h * width, width)] = rows[
                k * slots : (k + 1) * slots
            ]

    parts = [lambda span, ref=ref: ref[span, :] for ref in far]
    head_values(parts, value_ref, slots, out)
    multiply_tiles(range(len(order)), tiles, head_ref, keep_ref, send_ref)


def project_first(order, near, far, values, weight, columns, tile=512):
    depth, rows = weight.shape[0], 2 * near.shape[0]
    half = jax.ShapeDtypeStruct((rows // 2, columns), jnp.bfloat16)
    vmem = pl.BlockSpec(memory_space=pltpu.VMEM)
    return pl.pallas_call(
        functools.partial(project_first_kernel, order),
        out_shape=(jax.ShapeDtypeStruct((rows, depth), jnp.bfloat16), half, half),
        in_specs=[vmem] * (2 + len(far)) + [pl.BlockSpec(memory_space=pltpu.HBM)],
        name="project_first",
        **project_options(rows, depth, columns, tile),
    )(near, *far, values, in_hbm(weight))


def project_kernel(column, places, rows_ref, weight_ref, keep_ref, send_ref, tiles_ref, sems):
    multiply_tiles(places, stream(weight_ref, tiles_ref, sems, column), rows_ref, keep_ref, send_ref)


def project_options(rows, depth, columns, tile):
    return dict(
        scratch_shapes=[
            pltpu.VMEM((columns // tile, depth, tile), jnp.bfloat16),
            pltpu.SemaphoreType.DMA((columns // tile,)),
        ],
        compiler_params=pltpu.CompilerParams(vmem_limit_bytes=12 * MIB),
        cost_estimate=pl.CostEstimate(
            flops=2 * rows * depth * columns,
            bytes_accessed=2 * depth * columns + 2 * rows * (columns + depth),
            transcendentals=0,
        ),
    )


def project(rows, weight, columns, chunk, places, name, tile=512):
    count, depth = rows.shape
    half = jax.ShapeDtypeStruct((count // 2, columns), jnp.bfloat16)
    return pl.pallas_call(
        functools.partial(project_kernel, chunk * columns, tuple(places)),
        out_shape=(half, half),
        in_specs=[pl.BlockSpec(memory_space=pltpu.VMEM), pl.BlockSpec(memory_space=pltpu.HBM)],
        name=name,
        **project_options(count, depth, columns, tile),
    )(rows, in_hbm(weight))


def halve_kernel(keep_ref, came_ref, own_ref, send_ref):
    total = keep_ref[...].astype(jnp.float32) + came_ref[...].astype(jnp.float32)
    half = own_ref.shape[0]
    own_ref[...] = total[:half]
    send_ref[...] = total[half:].astype(send_ref.dtype)


def halve(keep, came):
    shape = (keep.shape[0] // 2, keep.shape[1])
    return pl.pallas_call(
        halve_kernel,
        out_shape=(
            jax.ShapeDtypeStruct(shape, jnp.float32),
            jax.ShapeDtypeStruct(shape, jnp.bfloat16),
        ),
        compiler_params=pltpu.CompilerParams(vmem_limit_bytes=6 * MIB),
        name="halve",
    )(keep, came)


def finish_kernel(residual_ref, gain_ref, own_ref, *refs):
    others, (middle_ref, scaled_ref) = refs[:-2], refs[-2:]
    middle = residual_ref[...].astype(jnp.float32) + own_ref[...]
    for other in others:
        middle = middle + other[...].astype(jnp.float32)
    middle_ref[...] = middle
    scaled_ref[...] = (middle * gain_ref[...]).astype(scaled_ref.dtype)


def finish_middle(residual, gain, sums, chunk):
    rows, columns = sums[0].shape
    here = lambda _: (0, chunk)
    block = pl.BlockSpec((rows, columns), lambda _: (0, 0))
    return pl.pallas_call(
        finish_kernel,
        out_shape=(
            jax.ShapeDtypeStruct((rows, columns), jnp.float32),
            jax.ShapeDtypeStruct((rows, columns), jnp.bfloat16),
        ),
        grid=(1,),
        in_specs=[pl.BlockSpec((rows, columns), here), pl.BlockSpec((1, columns), here)]
        + [block] * len(sums),
        out_specs=(block, block),
        compiler_params=pltpu.CompilerParams(vmem_limit_bytes=4 * MIB),
        name="finish_middle",
    )(residual, gain, *sums)


def gather_matmul_kernel(row, first, last, n_pieces, places, mean_over, *refs):
    pieces, refs = refs[:n_pieces], refs[n_pieces:]
    inverse_ref, gate_ref, up_ref, refs = refs[0], refs[1], refs[2], refs[3:]
    before, refs = ((), refs[1:]) if first else (refs[:3], refs[4:])
    if last:
        hidden_ref, gate_acc, up_acc, squares, *refs = refs
    else:
        gate_acc, up_acc, squares, *refs = refs
    rows_ref, tiles_ref, sems = refs
    steps, _, depth = rows_ref.shape
    copies = [
        pltpu.make_async_copy(
            up_ref.at[pl.ds(row + k * depth, depth), :], tiles_ref.at[k], sems.at[k]
        )
        for k in range(steps)
    ]
    for copy in copies:
        copy.start()
    size = pieces[0].shape[0]
    sources = [(piece, b) for piece in pieces for b in range(piece.shape[0] // size)]
    for (piece, b), place in zip(sources, places):
        for k in range(steps):
            rows_ref[k, pl.ds(place * size, size), :] = piece[
                pl.ds(b * size, size), pl.ds(k * depth, depth)
            ]
    for now, old in zip((gate_acc, up_acc, squares), before):
        now[...] = old[...]

    for k in range(steps):
        rows = rows_ref[k]
        plain = rows.astype(jnp.float32) * inverse_ref[:, pl.ds(k * depth, depth)]
        square = jnp.broadcast_to(jnp.sum(plain * plain, axis=1, keepdims=True), squares.shape)
        span = pl.ds(row + k * depth, depth)
        gate = jnp.dot(rows, gate_ref[span, :], preferred_element_type=jnp.float32)
        copies[k].wait()
        up = jnp.dot(rows, tiles_ref[k], preferred_element_type=jnp.float32)
        if first and k == 0:
            squares[...], gate_acc[...], up_acc[...] = square, gate, up
        else:
            squares[...] += square
            gate_acc[...] += gate
            up_acc[...] += up

    if last:
        factor = lax.rsqrt(squares[:, :1] / mean_over + 1e-06)
        gate = gate_acc[...] * factor
        hidden_ref[...] = (gate * jax.nn.sigmoid(gate) * (up_acc[...] * factor)).astype(
            jnp.bfloat16
        )


def gather_matmul(
    pieces, places, inverse_gain, gate_proj, up_proj, before, chunk, last, after, tile=512
):
    columns = pieces[0].shape[1]
    rows = sum(piece.shape[0] for piece in pieces)
    width, units = gate_proj.shape
    steps = columns // tile
    sums = ((rows, units), (rows, units), (rows, 128))
    if last:
        out_shape = jax.ShapeDtypeStruct((rows, units), jnp.bfloat16)
        scratch = [pltpu.VMEM(shape, jnp.float32) for shape in sums]
    else:
        out_shape = tuple(jax.ShapeDtypeStruct(shape, jnp.float32) for shape in sums)
        scratch = []
    vmem = pl.BlockSpec(memory_space=pltpu.VMEM)
    return pl.pallas_call(
        functools.partial(
            gather_matmul_kernel,
            chunk * columns,
            before is None,
            last,
            len(pieces),
            tuple(places),
            width,
        ),
        out_shape=out_shape,
        in_specs=[vmem] * (len(pieces) + 2)
        + [pl.BlockSpec(memory_space=pltpu.HBM)]
        + [vmem] * len(before or ())
        + [pl.BlockSpec(memory_space=pl.ANY)],
        scratch_shapes=scratch
        + [
            pltpu.VMEM((steps, rows, tile), jnp.bfloat16),
            pltpu.VMEM((steps, tile, units), jnp.bfloat16),
            pltpu.SemaphoreType.DMA((steps,)),
        ],
        compiler_params=pltpu.CompilerParams(vmem_limit_bytes=12 * MIB),
        cost_estimate=pl.CostEstimate(
            flops=4 * rows * columns * units,
            bytes_accessed=4 * columns * units + 2 * rows * columns,
            transcendentals=0,
        ),
        name="gate_up",
    )(*pieces, inverse_gain, in_vmem(gate_proj), in_hbm(up_proj), *(before or ()), after)


class Grid:
    def __init__(self, count):
        self.count = count
        self.bits = count.bit_length() - 1

    def dims(self, chunk):
        first = [1, 0] if chunk % 2 else [0, 1]
        return first + list(range(2, self.bits))

    def order(self, chunk):
        dims = self.dims(chunk)
        return [
            sum(1 << d for i, d in enumerate(dims) if n >> (self.bits - 1 - i) & 1)
            for n in range(self.count)
        ]

    def places(self, chunk):
        base = self.order(0)
        return [base.index(k) for k in self.order(chunk)]

    def exchange(self, array, k):
        return lax.ppermute(array, "dp", [(i, i ^ k) for i in range(self.count)])

    def exchange_near(self, array):
        half = self.count // 2
        groups = [list(range(half)), list(range(half, self.count))]
        return lax.all_to_all(
            array, "dp", split_axis=0, concat_axis=0, axis_index_groups=groups, tiled=True
        )

    def scatter_sum(self, keep, send, chunk):
        *before, last = self.dims(chunk)
        for d in before:
            keep, send = halve(keep, self.exchange(send, 1 << d))
        return [keep, self.exchange(send, 1 << last)]

    def gather(self, block, chunk):
        pieces = [block]
        for d in reversed(self.dims(chunk)):
            held = jnp.concatenate(pieces, axis=0) if len(pieces) > 1 else block
            pieces.append(self.exchange(held, 1 << d))
        return pieces


def add_up(base, parts):
    for part in parts:
        base = base + part.astype(jnp.float32)
    return base


def body(
    page_pool,
    move_source,
    move_page,
    move_slot,
    row_count,
    lengths,
    page_table,
    queries,
    value_up,
    out_proj,
    residual,
    norm_gain,
    gate_proj,
    up_proj,
    down_proj,
):
    rank_count = lax.axis_size("dp")
    own_rank = lax.axis_index("dp")
    grid = Grid(rank_count)
    rank = own_rank[None]
    move_count = move_page.shape[0] // rank_count
    capacity = max(2, (3 * move_count + 2 * rank_count - 1) // (2 * rank_count))
    slot_count, page_size, feature_width = page_pool.shape
    sources = move_source.T.reshape(rank_count, move_count)
    page_ids = move_page.reshape(rank_count, move_count)
    slot_ids = move_slot.reshape(rank_count, move_count)
    move_order = jnp.arange(move_count)
    earlier = (sources[:, :, None] == sources[:, None, :]) & (
        move_order[None, None, :] < move_order[None, :, None]
    )
    arrival = jnp.sum(earlier.astype(jnp.int32), axis=2)
    split = rank_count // 2
    far_peers = range(split, rank_count)
    pack = functools.partial(pack_pages, page_pool, move_source.T, move_page, rank, rank_count)
    packed = pack(far_peers, False, capacity, rank)
    far_pages = [grid.exchange(pages, k) for k, pages in zip(far_peers, packed)]
    (packed,) = pack(range(split), True, capacity, packed[0])
    near_pages = grid.exchange_near(packed)

    pick = lambda array: lax.dynamic_index_in_dim(array, own_rank, 0, keepdims=False)
    own_slots, own_pages = pick(slot_ids), pick(page_ids)
    peer = pick(sources) ^ own_rank
    place = jnp.where(peer < split, pick(sources) & (split - 1), peer) * capacity + pick(arrival)
    content_of = jnp.where(peer == 0, own_pages, slot_count + place)
    hit = page_table[:, :, None] == own_slots[None, None, :]
    content = jnp.where(
        jnp.any(hit, axis=2), jnp.sum(jnp.where(hit, content_of, 0), axis=2), page_table
    )
    places = slot_count + rank_count * capacity
    counts = slot_counts(content, lengths, jnp.arange(places), page_size)
    far_place = slot_count + split * capacity

    row_slots, head_count = queries.shape[:2]
    by_head_queries = queries.transpose(1, 0, 2).reshape(head_count * row_slots, feature_width)
    state = attend_resident(
        by_head_queries,
        page_pool.reshape(slot_count * page_size, feature_width),
        counts,
        page_size,
    )
    near_pages = near_pages.reshape((split * capacity,) + near_pages.shape[2:])
    state = attend_near(by_head_queries, [near_pages], counts, slot_count, state, page_size)
    far_latents, near_latents, ready = latents(
        by_head_queries,
        far_pages,
        counts,
        far_place,
        state,
        rank,
        row_count,
        page_size,
        rank_count,
        grid.exchange,
    )
    near_latents = grid.exchange_near(near_latents.reshape(split, -1, LATENT))

    width = residual.shape[1]
    columns = width // CHUNKS
    places = [grid.places(c) for c in range(CHUNKS)]
    values = value_up.reshape(-1, value_up.shape[2])
    values = preload(values, 0, values.shape[1], ready, LARGE, values.shape[1])
    near_heads = value_near(rank, near_latents, values)
    head_out, *halves = project_first(
        grid.order(0), near_heads, far_latents, values, out_proj, columns
    )
    projected = [halves] + [
        project(head_out, out_proj, columns, c, places[c], "project_out") for c in range(1, CHUNKS)
    ]
    middle, gathered = [], []
    for c, (keep, send) in enumerate(projected):
        row_sum, scaled = finish_middle(
            residual, norm_gain[None, :], grid.scatter_sum(keep, send, c), c
        )
        middle.append(row_sum)
        gathered.append(grid.gather(scaled, c))
    down_first = preload(
        down_proj,
        0,
        columns,
        gathered[-1][0],
        pl.CostEstimate(
            flops=0, bytes_accessed=2 * down_proj.shape[0] * columns, transcendentals=0
        ),
    )
    inverse_gain = (1.0 / norm_gain)[None, :]
    sums = None
    for c, pieces in enumerate(gathered):
        span = slice(c * columns, (c + 1) * columns)
        sums = gather_matmul(
            pieces,
            places[c],
            inverse_gain[:, span],
            gate_proj,
            up_proj,
            sums,
            c,
            c == CHUNKS - 1,
            down_first,
        )
    hidden = sums
    projected = [project_held(hidden, down_first, places[0], "project_down")] + [
        project(hidden, down_proj, columns, c, places[c], "project_down") for c in range(1, CHUNKS)
    ]
    outputs = [
        add_up(middle[c], grid.scatter_sum(keep, send, c)).astype(jnp.bfloat16)
        for c, (keep, send) in enumerate(projected)
    ]
    return jnp.concatenate(outputs, axis=1)


def solution(mesh):
    in_specs = (
        P(("rep", "dp"), None, None),
        P("rep", None),
        P("rep"),
        P("rep"),
        P(("rep", "dp")),
        P(("rep", "dp")),
        P(("rep", "dp"), None),
        P(("rep", "dp"), None, None),
        P("dp", None, None),
        P("dp", None),
        P(("rep", "dp"), None),
        P(),
        P(None, "dp"),
        P(None, "dp"),
        P("dp", None),
    )
    out_specs = P(("rep", "dp"), None)
    return jax.shard_map(body, mesh=mesh, in_specs=in_specs, out_specs=out_specs, check_vma=False)
```
